512 devices in a mesh: ctx: 64 (over z, x, core), kvh: 8 (over y).
Axes of the slice: x: 4, y: 8, z: 8, core: 2. Of those that a mesh axis runs over, the one named last changes fastest.
Arguments:
- queries: bfloat16 [512, 16384], P('ctx', 'kvh'), may hold values from -120 to 120
- keys: bfloat16 [262144, 1024], P('ctx', 'kvh'), may hold values from -6 to 6
- values: bfloat16 [262144, 1024], P('ctx', 'kvh'), may hold values from -6 to 6
- block_slots: int32 [512], replicated, may hold values from 0 to 511, as said below
- selected: int32 [8, 4, 64], replicated, may hold values from 0 to 511, as said below
- out_weight: bfloat16 [16384, 16384], P('kvh', 'ctx'), may hold values from -0.046875 to 0.046875
Outputs:
- projected: float32 [512, 16384], P('kvh', 'ctx')
The draws below stay inside these ranges and needn't reach their ends.
Inputs may be any that keep to these rules, and one draw needn't show every extreme that they name: `block_slots`: a permutation of the 512 logical blocks. selected[k, c] names 64 distinct logical blocks, block 511 always among them.
All inputs are finite; a program needn't handle non-finite values.
Results may differ from the reference program's by a relative error of at most 0.013.
Values may be sent and summed in bfloat16 or wider, within the bound.
No kernel may reach another device: no remote copies, remote signals or barrier semaphores. Data moves between devices by JAX's collectives and lax.ppermute only.
A program may use at most 64 MiB of HBM per device.

```python
import math
import jax
import jax.numpy as jnp
from jax import lax

DH = 128
GROUP = 16
D = 16384
BLKSZ = 512
QBLK = 128
NQB = 4
TOPK = 64
KVH = 8
H = 128
QTOK = 512
NBLK = 512


def shared_slots(key):
    return jax.random.permutation(jax.random.fold_in(key, 7), NBLK).astype(jnp.int32)


def draw_block_slots(key, part):
    return shared_slots(key)


def draw_queries(key, part):
    key = jax.random.fold_in(key, 4)
    return jax.random.truncated_normal(key, -6.0, 6.0, (QTOK, KVH * GROUP * DH), jnp.float32).astype(jnp.bfloat16)


def draw_keys(key, part):
    key = jax.random.fold_in(key, 5)
    return jax.random.truncated_normal(key, -6.0, 6.0, (NBLK * BLKSZ, KVH * DH), jnp.float32).astype(jnp.bfloat16)


def draw_selected(key, part):
    key = jax.random.fold_in(key, 3)
    popular_count = max(NBLK // 8, TOPK)
    order = jax.random.permutation(jax.random.fold_in(key, 1), NBLK - 1).astype(jnp.int32)
    popular = order[:popular_count]
    others = order[popular_count:]
    take_popular = TOPK // 2
    take_others = TOPK - take_popular - 1
    others_count = NBLK - 1 - popular_count
    score_popular = jax.random.randint(jax.random.fold_in(key, 2), (KVH, NQB, popular_count), 0, 1 << 20) * popular_count + jnp.arange(popular_count, dtype=jnp.int32)
    score_others = jax.random.randint(jax.random.fold_in(key, 3), (KVH, NQB, others_count), 0, 1 << 20) * others_count + jnp.arange(others_count, dtype=jnp.int32)
    _, pick_popular = lax.top_k(score_popular, take_popular)
    _, pick_others = lax.top_k(score_others, take_others)
    current = jnp.full((KVH, NQB, 1), NBLK - 1, jnp.int32)
    return jnp.concatenate([popular[pick_popular], others[pick_others], current], axis=2).astype(jnp.int32)


def shard_levels(stream_key, shape, cuts, smallest, largest):
    loudness, own = 1.0, jax.random.fold_in(stream_key, 6)
    for axis_at, shards_of in cuts:
        heights = jnp.exp(jax.random.uniform(jax.random.fold_in(own, axis_at), (shards_of,), jnp.float32, smallest / len(cuts), largest / len(cuts)))
        loudness = loudness * jnp.repeat(heights, shape[axis_at] // shards_of).reshape([-1 if axis == axis_at else 1 for axis in range(len(shape))])
    return loudness


def gaussian(own_key, shape, scale, limit, split=(), kind=jnp.bfloat16):
    values = scale * jax.random.normal(own_key, shape, jnp.float32)
    if split:
        values = values * shard_levels(own_key, shape, split, -0.22, 0.18)
    return jnp.clip(values, -limit, limit).astype(kind)


def setup_inputs(seed: int = 0) -> dict:
    streams_of = jax.random.split(jax.random.key(seed), 7)
    queries = draw_queries(jax.random.fold_in(streams_of[6], 71), 0)
    keys = draw_keys(jax.random.fold_in(streams_of[6], 71), 0)
    values = gaussian(streams_of[2], (NBLK * BLKSZ, KVH * DH), 1.0, 6.0, ((0, 64), (1, 8)))
    block_slots = draw_block_slots(jax.random.fold_in(streams_of[6], 71), 0)
    selected = draw_selected(jax.random.fold_in(streams_of[6], 71), 0)
    out_weight = gaussian(streams_of[5], (H * DH, D), (H * DH) ** -0.5, 0.046875, ((0, 8), (1, 64)))
    return {"queries": queries, "keys": keys, "values": values, "block_slots": block_slots, "selected": selected, "out_weight": out_weight}


NEG = -1e+30

def reference(queries, keys, values, block_slots, selected, out_weight):
    slot_of = jnp.zeros((NBLK,), jnp.int32).at[block_slots].set(jnp.arange(NBLK, dtype=jnp.int32))
    scale = 1.0 / math.sqrt(DH)
    lists = selected.reshape(KVH * NQB, TOPK)
    indices = jnp.arange(KVH * NQB, dtype=jnp.int32)

    def one_group(inputs):
        index, blocks = inputs
        head = index // NQB
        qblock = index % NQB
        first = (qblock * QBLK).astype(jnp.int32)
        qrows = lax.dynamic_slice(queries, (first, (head * GROUP * DH).astype(jnp.int32)), (QBLK, GROUP * DH))
        qrows = qrows.reshape(QBLK, GROUP, DH).astype(jnp.float32)
        qpos = BLKSZ - QTOK + first + jnp.arange(QBLK, dtype=jnp.int32)
        kpos = jnp.arange(BLKSZ, dtype=jnp.int32)

        def step(carry, block):
            top, total, acc = carry
            start = (slot_of[block] * BLKSZ).astype(jnp.int32)
            column = (head * DH).astype(jnp.int32)
            kblk = lax.dynamic_slice(keys, (start, column), (BLKSZ, DH)).astype(jnp.float32)
            vblk = lax.dynamic_slice(values, (start, column), (BLKSZ, DH)).astype(jnp.float32)
            scores = jnp.einsum('rgd,kd->rgk', qrows, kblk) * scale
            visible = (block != NBLK - 1) | (kpos[None, :] <= qpos[:, None])
            scores = jnp.where(visible[:, None, :], scores, NEG)
            new_top = jnp.maximum(top, lax.optimization_barrier(jnp.max(scores, axis=2)))
            probs = jnp.exp(scores - new_top[:, :, None])
            fade = jnp.exp(top - new_top)
            total = total * fade + lax.optimization_barrier(jnp.sum(probs, axis=2))
            rounded = lax.optimization_barrier(probs.astype(jnp.bfloat16))
            weights = rounded.astype(jnp.float32)
            acc = acc * fade[:, :, None] + jnp.einsum('rgk,kd->rgd', weights, vblk)
            return ((new_top, total, acc), None)
        start_state = (jnp.full((QBLK, GROUP), NEG, jnp.float32), jnp.zeros((QBLK, GROUP), jnp.float32), jnp.zeros((QBLK, GROUP, DH), jnp.float32))
        (top, total, acc), _ = lax.scan(step, start_state, blocks)
        return (acc / total[:, :, None]).reshape(QBLK, GROUP * DH).astype(jnp.bfloat16)
    pieces = lax.map(one_group, (indices, lists))
    attended = pieces.reshape(KVH, NQB, QBLK, GROUP * DH).transpose(1, 2, 0, 3).reshape(QTOK, H * DH)
    return jnp.dot(attended, out_weight, preferred_element_type=jnp.float32)
```

```python
import math

import jax
import jax.numpy as jnp
import numpy as np
from jax import lax
from jax.experimental import pallas as pl
from jax.experimental.pallas import tpu as pltpu
from jax.sharding import PartitionSpec as P

DH = 128
GROUP = 16
BLKSZ = 512
QBLK = 128
NQB = 4
ZN = 8
XN = 4
YN = 8
ROWS = 8
WIDE = GROUP * DH
STATE = WIDE + 128
SCALE = math.log2(math.e) / math.sqrt(DH)
NEG = -(2.0**100)
VMEM_LIMIT = 48 * 1024 * 1024
F32 = jnp.float32
BF16 = jnp.bfloat16


def place(z, x, core):
    return (z * XN + x) * 2 + core


Z_GROUPS = [[place(z, x, c) for z in range(ZN)] for x in range(XN) for c in range(2)]
X_GROUPS = [[place(z, x, c) for x in range(XN)] for z in range(ZN) for c in range(2)]
YC_GROUPS = [
    [place(z, x, c) * YN + y for c in range(2) for y in range(YN)]
    for z in range(ZN)
    for x in range(XN)
]
CORE_SWAP = [(place(z, x, c), place(z, x, 1 - c)) for z in range(ZN) for x in range(XN) for c in range(2)]


def exchange(blocks, axis, groups):
    return lax.all_to_all(
        blocks, axis, split_axis=0, concat_axis=0, tiled=True, axis_index_groups=groups
    )


def spread(rows, axis, groups):
    count = len(groups[0])
    return exchange(jnp.broadcast_to(rows[None], (count,) + rows.shape), axis, groups)


def in_vmem():
    return pl.BlockSpec(memory_space=pltpu.VMEM)


def in_smem():
    return pl.BlockSpec(memory_space=pltpu.SMEM)


def attend_kernel(hits_ref, core_ref, q_ref, k0_ref, v0_ref, k1_ref, v1_ref, out_ref, top, total, acc):
    tile = GROUP * 16
    blocks = k0_ref.shape[0] // BLKSZ
    core = core_ref[0]

    def one_block(c, k_ref, v_ref, b, masked):
        start = pl.multiple_of(b * BLKSZ, BLKSZ)
        kblk = k_ref[pl.ds(start, BLKSZ), :]
        vblk = v_ref[pl.ds(start, BLKSZ), :]
        for x in range(XN):
            qt = jnp.concatenate(
                [q_ref[x, c, :, h * DH : (h + 1) * DH] for h in range(GROUP)], axis=0
            )
            scores = (
                lax.dot_general(qt, kblk, (((1,), (1,)), ((), ())), preferred_element_type=F32)
                * SCALE
            )
            if masked:
                row = lax.broadcasted_iota(jnp.int32, (tile, BLKSZ), 0) % 16
                token = (((2 * c + row // 8) * XN + x) * 2 + core) * ROWS + row % 8
                kpos = lax.broadcasted_iota(jnp.int32, (tile, BLKSZ), 1)
                scores = jnp.where(kpos <= token, scores, NEG)
            old_top = top[x]
            new_top = jnp.maximum(old_top, jnp.max(scores, axis=1, keepdims=True))
            fade = jnp.exp2(old_top - new_top)
            parts = []
            added = None
            for j in range(BLKSZ // 128):
                part = jnp.exp2(scores[:, j * 128 : (j + 1) * 128] - new_top)
                added = part if added is None else added + part
                parts.append(part.astype(BF16))
            probs = jnp.concatenate(parts, axis=1)
            top[x] = new_top
            total[x] = total[x] * fade + added
            acc[x] = acc[x] * fade + jnp.dot(probs, vblk, preferred_element_type=F32)

    def query_block(c, carry):
        top[...] = jnp.full(top.shape, NEG, F32)
        total[...] = jnp.zeros(total.shape, F32)
        acc[...] = jnp.zeros(acc.shape, F32)
        for side, (k_ref, v_ref) in enumerate(((k0_ref, v0_ref), (k1_ref, v1_ref))):

            def step(b, carry, side=side, k_ref=k_ref, v_ref=v_ref):
                kind = hits_ref[c, side * blocks + b]

                @pl.when(kind == 1)
                def _():
                    one_block(c, k_ref, v_ref, b, False)

                @pl.when(kind == 2)
                def _():
                    one_block(c, k_ref, v_ref, b, True)

                return carry

            lax.fori_loop(0, blocks, step, 0)
        first = pl.multiple_of(c * 16, 16)
        lane = lax.broadcasted_iota(jnp.int32, (16, 128), 1)
        for x in range(XN):
            peak = top[x]
            kept = peak.astype(BF16).astype(F32)
            factor = jnp.exp2(peak - kept)
            scaled = (acc[x] * factor).astype(BF16)
            summed = jnp.sum(total[x], axis=1, keepdims=True) * factor
            high = summed.astype(BF16).astype(F32)
            low = summed - high
            stats = jnp.zeros((16, 128), F32)
            for h in range(GROUP):
                rows = slice(h * 16, (h + 1) * 16)
                out_ref[x, pl.ds(first, 16), h * DH : (h + 1) * DH] = scaled[rows]
                stats = jnp.where(lane == h, kept[rows], stats)
                stats = jnp.where(lane == GROUP + h, high[rows], stats)
                stats = jnp.where(lane == 2 * GROUP + h, low[rows], stats)
            out_ref[x, pl.ds(first, 16), WIDE:] = stats.astype(BF16)
        return carry

    lax.fori_loop(0, NQB, query_block, 0)


def attend(hits, core, q, k0, v0, k1, v1):
    tile = GROUP * 16
    return pl.pallas_call(
        attend_kernel,
        out_shape=jax.ShapeDtypeStruct((XN, NQB * 16, STATE), BF16),
        in_specs=[in_smem(), in_smem()] + [in_vmem()] * 5,
        out_specs=in_vmem(),
        scratch_shapes=[
            pltpu.VMEM((XN, tile, 128), F32),
            pltpu.VMEM((XN, tile, 128), F32),
            pltpu.VMEM((XN, tile, DH), F32),
        ],
        compiler_params=pltpu.CompilerParams(vmem_limit_bytes=VMEM_LIMIT),
    )(hits, core, q, k0, v0, k1, v1)


def weights_of(stats):
    tops = [s[:, :GROUP] for s in stats]
    peak = tops[0]
    for t in tops[1:]:
        peak = jnp.maximum(peak, t)
    weights = [jnp.exp2(t - peak) for t in tops]
    total = None
    for w, s in zip(weights, stats):
        term = w * (s[:, GROUP : 2 * GROUP] + s[:, 2 * GROUP : 3 * GROUP])
        total = term if total is None else total + term
    return peak, weights, total


def merge_kernel(in_ref, out_ref):
    count, rows = in_ref.shape[0], in_ref.shape[1]
    for r in range(0, rows, 16):
        stats = [in_ref[s, r : r + 16, WIDE:].astype(F32) for s in range(count)]
        peak, weights, total = weights_of(stats)
        for h in range(GROUP):
            cols = slice(h * DH, (h + 1) * DH)
            value = None
            for s in range(count):
                term = in_ref[s, r : r + 16, cols].astype(F32) * weights[s][:, h : h + 1]
                value = term if value is None else value + term
            out_ref[r : r + 16, cols] = value.astype(BF16)
        high = total.astype(BF16).astype(F32)
        rest = jnp.zeros((16, 128 - 3 * GROUP), F32)
        out_ref[r : r + 16, WIDE:] = jnp.concatenate([peak, high, total - high, rest], axis=1).astype(BF16)


def merge(states):
    return pl.pallas_call(
        merge_kernel,
        out_shape=jax.ShapeDtypeStruct(states.shape[1:], BF16),
        in_specs=[in_vmem()],
        out_specs=in_vmem(),
        compiler_params=pltpu.CompilerParams(vmem_limit_bytes=VMEM_LIMIT),
    )(states)


def finish_kernel(in_ref, out_ref):
    pairs = in_ref.shape[0] // 16
    stats = []
    for i in range(pairs):
        both = in_ref[i * 16 : (i + 1) * 16, WIDE:].astype(F32)
        stats += [both[:ROWS], both[ROWS:]]
    _, weights, total = weights_of(stats)
    inverse = 1.0 / total
    weights = [w * inverse for w in weights]
    for h in range(GROUP):
        cols = slice(h * DH, (h + 1) * DH)
        value = None
        for i in range(pairs):
            both = in_ref[i * 16 : (i + 1) * 16, cols].astype(F32)
            term = (
                both[:ROWS] * weights[2 * i][:, h : h + 1]
                + both[ROWS:] * weights[2 * i + 1][:, h : h + 1]
            )
            value = term if value is None else value + term
        twice = jnp.concatenate([value, value], axis=0).astype(BF16)
        for i in range(pairs):
            out_ref[i * 16 : (i + 1) * 16, cols] = twice


def finish(states):
    return pl.pallas_call(
        finish_kernel,
        out_shape=jax.ShapeDtypeStruct((ZN * ROWS, WIDE), BF16),
        in_specs=[in_vmem()],
        out_specs=in_vmem(),
        compiler_params=pltpu.CompilerParams(vmem_limit_bytes=VMEM_LIMIT),
    )(states)


def project_kernel(core_ref, a_ref, w0_ref, w1_ref, out_ref):
    core = core_ref[0]
    rows = a_ref[...].reshape(XN * ZN * ROWS, WIDE)
    for side, w_ref in enumerate((w0_ref, w1_ref)):
        result = jnp.dot(rows, w_ref[...], preferred_element_type=F32)
        target = core if side == 0 else 1 - core
        for z in range(ZN):
            chunk = jnp.concatenate(
                [result[(x * ZN + z) * ROWS : (x * ZN + z + 1) * ROWS] for x in range(XN)], axis=0
            )
            out_ref[target, z] = chunk.astype(BF16)


def project(core, rows, w0, w1):
    return pl.pallas_call(
        project_kernel,
        out_shape=jax.ShapeDtypeStruct((2, ZN, XN * ROWS, w0.shape[1]), BF16),
        in_specs=[in_smem()] + [in_vmem()] * 3,
        out_specs=in_vmem(),
        compiler_params=pltpu.CompilerParams(vmem_limit_bytes=VMEM_LIMIT),
    )(core, rows, w0, w1)


def find_hits(block_slots, selected, device, head, local_blocks):
    chosen = lax.dynamic_index_in_dim(selected, head, 0, keepdims=False)
    pair = lax.dynamic_slice_in_dim(block_slots, device // 2 * 2 * local_blocks, 2 * local_blocks)
    pair = pair.reshape(2, local_blocks)
    logical = jnp.where(device % 2 == 0, pair, pair[::-1]).reshape(-1)
    hit = jnp.any(chosen[:, None, :] == logical[None, :, None], axis=2).astype(jnp.int32)
    last = (logical == block_slots.shape[0] - 1).astype(jnp.int32)
    return hit * (1 + last[None, :])


def body(queries, keys, values, block_slots, selected, out_weight):
    device = lax.axis_index("ctx")
    head = lax.axis_index("kvh")
    core = (device % 2).reshape(1).astype(jnp.int32)
    hits = find_hits(block_slots, selected, device, head, keys.shape[0] // BLKSZ)
    other_keys = lax.ppermute(keys, "ctx", CORE_SWAP)
    other_values = lax.ppermute(values, "ctx", CORE_SWAP)
    other_weight = lax.ppermute(out_weight, "ctx", CORE_SWAP)

    column = spread(queries, "ctx", Z_GROUPS).reshape(ZN * ROWS, WIDE)
    plane = spread(column, "ctx", X_GROUPS).reshape(XN, NQB, 16, WIDE)
    states = attend(hits, core, plane, keys, values, other_keys, other_values)
    merged = merge(exchange(states, "ctx", X_GROUPS))
    arrived = exchange(merged.reshape(ZN, ROWS, STATE), "ctx", Z_GROUPS)
    attended = finish(arrived.reshape(ZN * ROWS, STATE)).reshape(ZN, ROWS, WIDE)

    column = exchange(attended, "ctx", Z_GROUPS).reshape(ZN * ROWS, WIDE)
    plane = spread(column, "ctx", X_GROUPS)
    shares = project(core, plane, out_weight, other_weight)
    arrived = exchange(shares.reshape(2 * YN, XN * ROWS, -1), ("ctx", "kvh"), YC_GROUPS)
    summed = jnp.sum(arrived.reshape(2, YN, XN, ROWS, -1).astype(F32), axis=1)
    return jnp.swapaxes(summed, 0, 1).reshape(XN * 2 * ROWS, -1)


def solution(mesh):
    return jax.shard_map(
        body,
        mesh=mesh,
        in_specs=(P("ctx", "kvh"), P("ctx", "kvh"), P("ctx", "kvh"), P(), P(), P("kvh", "ctx")),
        out_specs=P("kvh", "ctx"),
        check_vma=False,
    )
```

```python
import functools
import math

import jax
import jax.numpy as jnp
from jax import lax
from jax.experimental import pallas as pl
from jax.experimental.pallas import tpu as pltpu
from jax.sharding import PartitionSpec as P

DH = 128
GROUP = 16
BLKSZ = 512
QBLK = 128
NQB = 4
ZN = 8
XN = 4
YN = 8
ROWS = 8
WIDE = GROUP * DH
STATE = WIDE + 128
SCALE = math.log2(math.e) / math.sqrt(DH)
NEG = -(2.0**100)
VMEM_LIMIT = 48 * 1024 * 1024
F32 = jnp.float32
BF16 = jnp.bfloat16


def place(z, x, core):
    return (z * XN + x) * 2 + core


Z_GROUPS = [[place(z, x, c) for z in range(ZN)] for x in range(XN) for c in range(2)]
X_GROUPS = [[place(z, x, c) for x in range(XN)] for z in range(ZN) for c in range(2)]
YC_GROUPS = [
    [place(z, x, c) * YN + y for c in range(2) for y in range(YN)]
    for z in range(ZN)
    for x in range(XN)
]
CORE_SWAP = [(place(z, x, c), place(z, x, 1 - c)) for z in range(ZN) for x in range(XN) for c in range(2)]


def exchange(blocks, axis, groups):
    return lax.all_to_all(
        blocks, axis, split_axis=0, concat_axis=0, tiled=True, axis_index_groups=groups
    )


def spread(rows, axis, groups):
    count = len(groups[0])
    return exchange(jnp.broadcast_to(rows[None], (count,) + rows.shape), axis, groups)


def in_vmem():
    return pl.BlockSpec(memory_space=pltpu.VMEM)


def in_smem():
    return pl.BlockSpec(memory_space=pltpu.SMEM)


def attend_kernel(
    alone,
    hits_ref,
    place_ref,
    q_ref,
    k0_ref,
    v0_ref,
    k1_ref,
    v1_ref,
    *rest,
):
    own_ref = None if alone else rest[0]
    out_ref, top, total, acc, scaled, k_all, v_all, listed, sems = rest[0 if alone else 1 :]
    tile = GROUP * 16
    local = k0_ref.shape[0]
    blocks = 2 * local // BLKSZ
    column = place_ref[0]
    core = place_ref[1]
    parts = [column] if alone else [lax.rem(column + j, XN) for j in range(1, XN)]
    copies = []
    for i, (source, target, start) in enumerate(
        ((k0_ref, k_all, 0), (v0_ref, v_all, 0), (k1_ref, k_all, local), (v1_ref, v_all, local))
    ):
        copy = pltpu.make_async_copy(source, target.at[pl.ds(start, local)], sems.at[i])
        copy.start()
        copies.append(copy)
    if not alone:
        out_ref[column] = own_ref[...]
    for copy in copies:
        copy.wait()

    def block_of(ref, b):
        return ref[pl.ds(pl.multiple_of(b * BLKSZ, BLKSZ), BLKSZ), :]

    def rows_of(i):
        return slice(i * tile, (i + 1) * tile)

    def score(i, group):
        kblk = jnp.concatenate([block_of(k_all, b) for b in group], axis=0)
        return lax.dot_general(
            scaled[rows_of(i)],
            jnp.concatenate([kblk, kblk], axis=1),
            (((1,), (1,)), ((), ())),
            preferred_element_type=F32,
        )

    def soften(i, scores):
        old_top = top[rows_of(i)]
        new_top = jnp.maximum(old_top, jnp.max(scores, axis=1, keepdims=True))
        fade = jnp.exp2(old_top - new_top)
        probs = []
        added = None
        for j in range(scores.shape[1] // 128):
            part = jnp.exp2(scores[:, j * 128 : (j + 1) * 128] - new_top)
            added = part if added is None else added + part
            probs.append(part.astype(BF16))
        top[rows_of(i)] = new_top
        total[rows_of(i)] = total[rows_of(i)] * fade + added
        return jnp.concatenate(probs, axis=1), fade

    def gather(i, group, probs, fade):
        vblk = jnp.concatenate([block_of(v_all, b) for b in group], axis=0)
        acc[rows_of(i)] = acc[rows_of(i)] * fade + jnp.dot(probs, vblk, preferred_element_type=F32)

    def run(work, mask=None):
        scores = score(*work[0])
        before = None
        for at, (i, group) in enumerate(work):
            following = score(*work[at + 1]) if at + 1 < len(work) else None
            if mask is not None:
                scores = jnp.where(mask(i), scores, NEG)
            probs, fade = soften(i, scores)
            if before is not None:
                gather(*before)
            before = (i, group, probs, fade)
            scores = following
        gather(*before)

    def query_block(c, carry):
        top[...] = jnp.full(top.shape, NEG, F32)
        total[...] = jnp.zeros(total.shape, F32)
        acc[...] = jnp.zeros(acc.shape, F32)
        for i, x in enumerate(parts):
            source = q_ref.at[c] if alone else q_ref.at[x, c]
            rows = jnp.concatenate([source[:, h * DH : (h + 1) * DH] for h in range(GROUP)], axis=0)
            rows = rows.astype(F32) * SCALE
            high = rows.astype(BF16)
            low = (rows - high.astype(F32)).astype(BF16)
            scaled[rows_of(i)] = jnp.concatenate([high, low], axis=1)

        def collect(b, found):
            listed[found] = b
            return found + jnp.where(hits_ref[c, b] == 1, 1, 0)

        found = lax.fori_loop(0, blocks, collect, 0)
        span = range(len(parts))

        def two(j, carry):
            first, second = listed[2 * j], listed[2 * j + 1]
            if alone:
                run([(i, [b]) for b in (first, second) for i in span])
            else:
                run([(i, [first, second]) for i in span])
            return carry

        lax.fori_loop(0, found // 2, two, 0)

        @pl.when(found % 2 == 1)
        def _():
            run([(i, [listed[found - 1]]) for i in span])

        def current(b, carry):
            @pl.when(hits_ref[c, b] == 2)
            def _():
                def mask(i):
                    row = lax.broadcasted_iota(jnp.int32, (tile, BLKSZ), 0) % 16
                    token = (((2 * c + row // 8) * XN + parts[i]) * 2 + core) * ROWS + row % 8
                    return lax.broadcasted_iota(jnp.int32, (tile, BLKSZ), 1) <= token

                run([(i, [b]) for i in span], mask)

            return carry

        lax.fori_loop(0, blocks, current, 0)

        first = pl.multiple_of(c * 16, 16)
        lane = lax.broadcasted_iota(jnp.int32, (16, 128), 1)
        for i, x in enumerate(parts):
            target = out_ref if alone else out_ref.at[x]
            peak = top[rows_of(i)]
            kept = peak.astype(BF16).astype(F32)
            factor = jnp.exp2(peak - kept)
            values = (acc[rows_of(i)] * factor).astype(BF16)
            summed = jnp.sum(total[rows_of(i)], axis=1, keepdims=True) * factor
            high = summed.astype(BF16).astype(F32)
            low = summed - high
            stats = jnp.zeros((16, 128), F32)
            for h in range(GROUP):
                rows = slice(h * 16, (h + 1) * 16)
                target[pl.ds(first, 16), h * DH : (h + 1) * DH] = values[rows]
                stats = jnp.where(lane == h, kept[rows], stats)
                stats = jnp.where(lane == GROUP + h, high[rows], stats)
                stats = jnp.where(lane == 2 * GROUP + h, low[rows], stats)
            target[pl.ds(first, 16), WIDE:] = stats.astype(BF16)
        return carry

    lax.fori_loop(0, NQB, query_block, 0)


def attend(alone, hits, where, q, k0, v0, k1, v1, own=None):
    parts = 1 if alone else XN - 1
    tile = GROUP * 16
    shape = (NQB * 16, STATE) if alone else (XN, NQB * 16, STATE)
    operands = (hits, where, q, k0, v0, k1, v1) + (() if alone else (own,))
    specs = [in_smem(), in_smem(), in_vmem()] + [pl.BlockSpec(memory_space=pl.ANY)] * 4
    specs += [] if alone else [in_vmem()]
    pairs = 8 * parts * tile * BLKSZ
    return pl.pallas_call(
        functools.partial(attend_kernel, alone),
        name="attend_own" if alone else "attend_rest",
        out_shape=jax.ShapeDtypeStruct(shape, BF16),
        in_specs=specs,
        out_specs=in_vmem(),
        scratch_shapes=[
            pltpu.VMEM((parts * tile, 128), F32),
            pltpu.VMEM((parts * tile, 128), F32),
            pltpu.VMEM((parts * tile, DH), F32),
            pltpu.VMEM((parts * tile, 2 * DH), BF16),
            pltpu.VMEM((2 * k0.shape[0], DH), BF16),
            pltpu.VMEM((2 * k0.shape[0], DH), BF16),
            pltpu.SMEM((2 * k0.shape[0] // BLKSZ + 8,), jnp.int32),
            pltpu.SemaphoreType.DMA((4,)),
        ],
        compiler_params=pltpu.CompilerParams(vmem_limit_bytes=VMEM_LIMIT),
        cost_estimate=pl.CostEstimate(
            flops=pairs * 4 * DH, bytes_accessed=8 * 1024 * 1024, transcendentals=pairs
        ),
    )(*operands)


def weights_of(stats):
    tops = [s[:, :GROUP] for s in stats]
    peak = tops[0]
    for t in tops[1:]:
        peak = jnp.maximum(peak, t)
    weights = [jnp.exp2(t - peak) for t in tops]
    total = None
    for w, s in zip(weights, stats):
        term = w * (s[:, GROUP : 2 * GROUP] + s[:, 2 * GROUP : 3 * GROUP])
        total = term if total is None else total + term
    return peak, weights, total


def merge_kernel(in_ref, out_ref):
    count, rows = in_ref.shape[0], in_ref.shape[1]
    for r in range(0, rows, 16):
        stats = [in_ref[s, r : r + 16, WIDE:].astype(F32) for s in range(count)]
        peak, weights, total = weights_of(stats)
        for h in range(GROUP):
            cols = slice(h * DH, (h + 1) * DH)
            value = None
            for s in range(count):
                term = in_ref[s, r : r + 16, cols].astype(F32) * weights[s][:, h : h + 1]
                value = term if value is None else value + term
            out_ref[r : r + 16, cols] = value.astype(BF16)
        high = total.astype(BF16).astype(F32)
        rest = jnp.zeros((16, 128 - 3 * GROUP), F32)
        out_ref[r : r + 16, WIDE:] = jnp.concatenate([peak, high, total - high, rest], axis=1).astype(BF16)


def merge(states):
    return pl.pallas_call(
        merge_kernel,
        out_shape=jax.ShapeDtypeStruct(states.shape[1:], BF16),
        in_specs=[in_vmem()],
        out_specs=in_vmem(),
        compiler_params=pltpu.CompilerParams(vmem_limit_bytes=VMEM_LIMIT),
    )(states)


def finish_kernel(in_ref, out_ref):
    pairs = in_ref.shape[0] // 16
    stats = []
    for i in range(pairs):
        both = in_ref[i * 16 : (i + 1) * 16, WIDE:].astype(F32)
        stats += [both[:ROWS], both[ROWS:]]
    _, weights, total = weights_of(stats)
    inverse = 1.0 / total
    weights = [w * inverse for w in weights]
    for h in range(GROUP):
        cols = slice(h * DH, (h + 1) * DH)
        value = None
        for i in range(pairs):
            both = in_ref[i * 16 : (i + 1) * 16, cols].astype(F32)
            term = (
                both[:ROWS] * weights[2 * i][:, h : h + 1]
                + both[ROWS:] * weights[2 * i + 1][:, h : h + 1]
            )
            value = term if value is None else value + term
        twice = jnp.concatenate([value, value], axis=0).astype(BF16)
        for i in range(pairs):
            out_ref[i * 16 : (i + 1) * 16, cols] = twice


def finish(states):
    return pl.pallas_call(
        finish_kernel,
        out_shape=jax.ShapeDtypeStruct((ZN * ROWS, WIDE), BF16),
        in_specs=[in_vmem()],
        out_specs=in_vmem(),
        compiler_params=pltpu.CompilerParams(vmem_limit_bytes=VMEM_LIMIT),
    )(states)


def project_kernel(core_ref, a_ref, w0_ref, w1_ref, out_ref):
    core = core_ref[0]
    rows = a_ref[...].reshape(XN * ZN * ROWS, WIDE)
    for side, w_ref in enumerate((w0_ref, w1_ref)):
        result = jnp.dot(rows, w_ref[...], preferred_element_type=F32)
        target = core if side == 0 else 1 - core
        for z in range(ZN):
            chunk = jnp.concatenate(
                [result[(x * ZN + z) * ROWS : (x * ZN + z + 1) * ROWS] for x in range(XN)], axis=0
            )
            out_ref[target, z] = chunk.astype(BF16)


def project(core, rows, w0, w1):
    return pl.pallas_call(
        project_kernel,
        out_shape=jax.ShapeDtypeStruct((2, ZN, XN * ROWS, w0.shape[1]), BF16),
        in_specs=[in_smem()] + [in_vmem()] * 3,
        out_specs=in_vmem(),
        compiler_params=pltpu.CompilerParams(vmem_limit_bytes=VMEM_LIMIT),
    )(core, rows, w0, w1)


def find_hits(block_slots, selected, device, head, local_blocks):
    chosen = lax.dynamic_index_in_dim(selected, head, 0, keepdims=False)
    pair = lax.dynamic_slice_in_dim(block_slots, device // 2 * 2 * local_blocks, 2 * local_blocks)
    pair = pair.reshape(2, local_blocks)
    logical = jnp.where(device % 2 == 0, pair, pair[::-1]).reshape(-1)
    hit = jnp.any(chosen[:, None, :] == logical[None, :, None], axis=2).astype(jnp.int32)
    last = (logical == block_slots.shape[0] - 1).astype(jnp.int32)
    return hit * (1 + last[None, :])


def body(queries, keys, values, block_slots, selected, out_weight):
    device = lax.axis_index("ctx")
    head = lax.axis_index("kvh")
    core = (device % 2).reshape(1).astype(jnp.int32)
    where = jnp.stack([device // 2 % XN, device % 2]).astype(jnp.int32)
    hits = find_hits(block_slots, selected, device, head, keys.shape[0] // BLKSZ)
    other_keys = lax.ppermute(keys, "ctx", CORE_SWAP)
    other_values = lax.ppermute(values, "ctx", CORE_SWAP)
    other_weight = lax.ppermute(out_weight, "ctx", CORE_SWAP)

    column = spread(queries, "ctx", Z_GROUPS).reshape(ZN * ROWS, WIDE)
    cache = (keys, values, other_keys, other_values)
    own = attend(True, hits, where, column.reshape(NQB, 16, WIDE), *cache)
    plane = spread(column, "ctx", X_GROUPS).reshape(XN, NQB, 16, WIDE)
    states = attend(False, hits, where, plane, *cache, own=own)
    merged = merge(exchange(states, "ctx", X_GROUPS))
    arrived = exchange(merged.reshape(ZN, ROWS, STATE), "ctx", Z_GROUPS)
    attended = finish(arrived.reshape(ZN * ROWS, STATE)).reshape(ZN, ROWS, WIDE)

    column = exchange(attended, "ctx", Z_GROUPS).reshape(ZN * ROWS, WIDE)
    plane = spread(column, "ctx", X_GROUPS)
    shares = project(core, plane, out_weight, other_weight)
    arrived = exchange(shares.reshape(2 * YN, XN * ROWS, -1), ("ctx", "kvh"), YC_GROUPS)
    summed = jnp.sum(arrived.reshape(2, YN, XN, ROWS, -1).astype(F32), axis=1)
    return jnp.swapaxes(summed, 0, 1).reshape(XN * 2 * ROWS, -1)


def solution(mesh):
    return jax.shard_map(
        body,
        mesh=mesh,
        in_specs=(P("ctx", "kvh"), P("ctx", "kvh"), P("ctx", "kvh"), P(), P(), P("kvh", "ctx")),
        out_specs=P("kvh", "ctx"),
        check_vma=False,
    )
```

```python
import functools
import math

import jax
import jax.numpy as jnp
from jax import lax
from jax.experimental import pallas as pl
from jax.experimental.pallas import tpu as pltpu
from jax.sharding import PartitionSpec as P

DH = 128
GROUP = 16
BLKSZ = 512
QBLK = 128
NQB = 4
ZN = 8
XN = 4
YN = 8
ROWS = 8
WIDE = GROUP * DH
STATE = WIDE + 128
SCALE = math.log2(math.e) / math.sqrt(DH)
NEG = -(2.0**100)
VMEM_LIMIT = 24 * 1024 * 1024
F32 = jnp.float32
BF16 = jnp.bfloat16


def place(z, x, core):
    return (z * XN + x) * 2 + core


Z_GROUPS = [[place(z, x, c) for z in range(ZN)] for x in range(XN) for c in range(2)]
X_GROUPS = [[place(z, x, c) for x in range(XN)] for z in range(ZN) for c in range(2)]
NEAR_GROUPS = [
    [place((2 * pair + low + c) % ZN, x, c) for low in range(2) for x in range(XN)]
    for pair in range(ZN // 2)
    for c in range(2)
]
FAR_GROUPS = [
    [place((2 * pair + low + c) % ZN, x, c) for pair in range(ZN // 2)]
    for low in range(2)
    for x in range(XN)
    for c in range(2)
]
YC_GROUPS = [
    [place(z, x, c) * YN + y for c in range(2) for y in range(YN)]
    for z in range(ZN)
    for x in range(XN)
]
CORE_SWAP = [(place(z, x, c), place(z, x, 1 - c)) for z in range(ZN) for x in range(XN) for c in range(2)]


def exchange(blocks, axis, groups):
    return lax.all_to_all(
        blocks, axis, split_axis=0, concat_axis=0, tiled=True, axis_index_groups=groups
    )


def spread(rows, axis, groups):
    count = len(groups[0])
    return exchange(jnp.broadcast_to(rows[None], (count,) + rows.shape), axis, groups)


def in_vmem():
    return pl.BlockSpec(memory_space=pltpu.VMEM)


def in_hbm():
    return pl.BlockSpec(memory_space=pltpu.HBM)


def in_smem():
    return pl.BlockSpec(memory_space=pltpu.SMEM)


def attend_kernel(alone, place_ref, q_ref, *rest):
    tile = GROUP * 16
    column = place_ref[0]
    core = place_ref[1]
    if alone:
        hits_ref, k0_ref, v0_ref, k1_ref, v1_ref, final_ref, listed, out_ref = rest[:8]
        parts = [column]
    else:
        listed, k0_ref, v0_ref, k1_ref, v1_ref, out_ref = rest[:6]
        parts = [lax.rem(column + j, XN) for j in range(1, XN)]
    top, total, acc, scaled, k_all, v_all, sems = rest[8 if alone else 6 :]
    local = k0_ref.shape[0]
    blocks = 2 * local // BLKSZ
    copies = []
    for i, (source, target, start) in enumerate(
        ((k0_ref, k_all, 0), (v0_ref, v_all, 0), (k1_ref, k_all, local), (v1_ref, v_all, local))
    ):
        copy = pltpu.make_async_copy(source, target.at[pl.ds(start, local)], sems.at[i])
        copy.start()
        copies.append(copy)

    if alone:

        def collect(c, carry):
            listed[c, blocks + 1] = -1

            def look(b, found):
                kind = hits_ref[c, b]
                listed[c, found] = b

                @pl.when(kind == 2)
                def _():
                    listed[c, blocks + 1] = b

                return found + jnp.where(kind == 1, 1, 0)

            listed[c, blocks] = lax.fori_loop(0, blocks, look, 0)
            return carry

        lax.fori_loop(0, NQB, collect, 0)

    def block_of(ref, b):
        return ref[pl.ds(pl.multiple_of(b * BLKSZ, BLKSZ), BLKSZ), :]

    def rows_of(i):
        return slice(i * tile, (i + 1) * tile)

    def score(i, group):
        kblk = jnp.concatenate([block_of(k_all, b) for b in group], axis=0)
        return lax.dot_general(
            scaled[rows_of(i)],
            jnp.concatenate([kblk, kblk], axis=1),
            (((1,), (1,)), ((), ())),
            preferred_element_type=F32,
        )

    def soften(i, scores):
        old_top = top[rows_of(i)]
        new_top = jnp.maximum(old_top, jnp.max(scores, axis=1, keepdims=True))
        fade = jnp.exp2(old_top - new_top)
        probs = []
        added = None
        for j in range(scores.shape[1] // 128):
            part = jnp.exp2(scores[:, j * 128 : (j + 1) * 128] - new_top)
            added = part if added is None else added + part
            probs.append(part.astype(BF16))
        top[rows_of(i)] = new_top
        total[rows_of(i)] = total[rows_of(i)] * fade + added
        return jnp.concatenate(probs, axis=1), fade

    def gather(i, group, probs, fade):
        vblk = jnp.concatenate([block_of(v_all, b) for b in group], axis=0)
        acc[rows_of(i)] = acc[rows_of(i)] * fade + jnp.dot(probs, vblk, preferred_element_type=F32)

    def run(work, mask=None):
        scores = score(*work[0])
        before = None
        for at, (i, group) in enumerate(work):
            following = score(*work[at + 1]) if at + 1 < len(work) else None
            if mask is not None:
                scores = jnp.where(mask(i), scores, NEG)
            probs, fade = soften(i, scores)
            if before is not None:
                gather(*before)
            before = (i, group, probs, fade)
            scores = following
        gather(*before)

    def prepare(c):
        top[...] = jnp.full(top.shape, NEG, F32)
        total[...] = jnp.zeros(total.shape, F32)
        acc[...] = jnp.zeros(acc.shape, F32)
        for i, x in enumerate(parts):
            source = q_ref.at[c] if alone else q_ref.at[x, c]
            rows = jnp.concatenate([source[:, h * DH : (h + 1) * DH] for h in range(GROUP)], axis=0)
            rows = rows.astype(F32) * SCALE
            high = rows.astype(BF16)
            low = (rows - high.astype(F32)).astype(BF16)
            scaled[rows_of(i)] = jnp.concatenate([high, low], axis=1)

    def query_block(c, carry):
        @pl.when(c > 0)
        def _():
            prepare(c)

        found = listed[c, blocks]
        current = listed[c, blocks + 1]
        span = range(len(parts))

        def two(j, carry):
            first, second = listed[c, 2 * j], listed[c, 2 * j + 1]
            if alone:
                run([(i, [b]) for b in (first, second) for i in span])
            else:
                run([(i, [first, second]) for i in span])
            return carry

        lax.fori_loop(0, found // 2, two, 0)

        @pl.when(found % 2 == 1)
        def _():
            run([(i, [listed[c, found - 1]]) for i in span])

        @pl.when(current >= 0)
        def _():
            def mask(i):
                row = lax.broadcasted_iota(jnp.int32, (tile, BLKSZ), 0) % 16
                token = (((2 * c + row // 8) * XN + parts[i]) * 2 + core) * ROWS + row % 8
                return lax.broadcasted_iota(jnp.int32, (tile, BLKSZ), 1) <= token

            run([(i, [current]) for i in span], mask)

        first = pl.multiple_of(c * 16, 16)
        lane = lax.broadcasted_iota(jnp.int32, (16, 128), 1)
        for i, x in enumerate(parts):
            target = out_ref if alone else out_ref.at[x]
            peak = top[rows_of(i)]
            kept = peak.astype(BF16).astype(F32)
            factor = jnp.exp2(peak - kept)
            values = (acc[rows_of(i)] * factor).astype(BF16)
            summed = jnp.sum(total[rows_of(i)], axis=1, keepdims=True) * factor
            high = summed.astype(BF16).astype(F32)
            low = summed - high
            stats = jnp.zeros((16, 128), F32)
            for h in range(GROUP):
                rows = slice(h * 16, (h + 1) * 16)
                target[pl.ds(first, 16), h * DH : (h + 1) * DH] = values[rows]
                stats = jnp.where(lane == h, kept[rows], stats)
                stats = jnp.where(lane == GROUP + h, high[rows], stats)
                stats = jnp.where(lane == 2 * GROUP + h, low[rows], stats)
            target[pl.ds(first, 16), WIDE:] = stats.astype(BF16)
        return carry

    prepare(0)
    for copy in copies:
        copy.wait()
    lax.fori_loop(0, NQB, query_block, 0)
    if alone:
        copy = pltpu.make_async_copy(out_ref, final_ref, sems.at[4])
        copy.start()
        copy.wait()


def state_scratch(parts, tokens):
    tile = parts * GROUP * 16
    return [
        pltpu.VMEM((tile, 128), F32),
        pltpu.VMEM((tile, 128), F32),
        pltpu.VMEM((tile, DH), F32),
        pltpu.VMEM((tile, 2 * DH), BF16),
        pltpu.VMEM((tokens, DH), BF16),
        pltpu.VMEM((tokens, DH), BF16),
        pltpu.SemaphoreType.DMA((5,)),
    ]


def attend_cost(parts):
    pairs = 8 * parts * GROUP * 16 * BLKSZ
    return pl.CostEstimate(flops=pairs * 4 * DH, bytes_accessed=8 * 1024 * 1024, transcendentals=pairs)


def attend_own(where, q, hits, cache):
    tokens = 2 * cache[0].shape[0]
    state = jax.ShapeDtypeStruct((NQB * 16, STATE), BF16)
    return pl.pallas_call(
        functools.partial(attend_kernel, True),
        name="attend_own",
        out_shape=(state, jax.ShapeDtypeStruct((NQB, tokens // BLKSZ + 8), jnp.int32)),
        in_specs=[in_smem(), in_vmem(), in_smem()] + [in_hbm()] * 4,
        out_specs=(in_hbm(), in_smem()),
        scratch_shapes=[pltpu.VMEM(state.shape, BF16)] + state_scratch(1, tokens),
        compiler_params=pltpu.CompilerParams(vmem_limit_bytes=VMEM_LIMIT),
        cost_estimate=attend_cost(1),
    )(where, q, hits, *cache)


def attend_rest(where, q, listed, cache):
    return pl.pallas_call(
        functools.partial(attend_kernel, False),
        name="attend_rest",
        out_shape=jax.ShapeDtypeStruct((XN, NQB * 16, STATE), BF16),
        in_specs=[in_smem(), in_vmem(), in_smem()] + [in_hbm()] * 4,
        out_specs=in_vmem(),
        scratch_shapes=state_scratch(XN - 1, 2 * cache[0].shape[0]),
        compiler_params=pltpu.CompilerParams(vmem_limit_bytes=VMEM_LIMIT),
        cost_estimate=attend_cost(XN - 1),
    )(where, q, listed, *cache)


def weights_of(stats):
    tops = [s[:, :GROUP] for s in stats]
    peak = tops[0]
    for t in tops[1:]:
        peak = jnp.maximum(peak, t)
    weights = [jnp.exp2(t - peak) for t in tops]
    total = None
    for w, s in zip(weights, stats):
        term = w * (s[:, GROUP : 2 * GROUP] + s[:, 2 * GROUP : 3 * GROUP])
        total = term if total is None else total + term
    return peak, weights, total


def merge_kernel(place_ref, own_ref, in_ref, out_ref):
    rows = own_ref.shape[0]
    column = place_ref[0]
    sources = [own_ref] + [in_ref.at[lax.rem(column + j, XN)] for j in range(1, XN)]
    peak, weights, total = weights_of([s[:, WIDE:].astype(F32) for s in sources])
    for h in range(GROUP):
        cols = slice(h * DH, (h + 1) * DH)
        value = None
        for source, weight in zip(sources, weights):
            term = source[:, cols].astype(F32) * weight[:, h : h + 1]
            value = term if value is None else value + term
        out_ref[:, cols] = value.astype(BF16)
    high = total.astype(BF16).astype(F32)
    rest = jnp.zeros((rows, 128 - 3 * GROUP), F32)
    out_ref[:, WIDE:] = jnp.concatenate([peak, high, total - high, rest], axis=1).astype(BF16)


def merge(where, own, states):
    return pl.pallas_call(
        merge_kernel,
        name="merge",
        out_shape=jax.ShapeDtypeStruct(states.shape[1:], BF16),
        in_specs=[in_smem(), in_vmem(), in_vmem()],
        out_specs=in_vmem(),
        compiler_params=pltpu.CompilerParams(vmem_limit_bytes=VMEM_LIMIT),
    )(where, own, states)


def finish_kernel(in_ref, out_ref):
    pairs = in_ref.shape[0] // 16
    stats = []
    for i in range(pairs):
        both = in_ref[i * 16 : (i + 1) * 16, WIDE:].astype(F32)
        stats += [both[:ROWS], both[ROWS:]]
    _, weights, total = weights_of(stats)
    inverse = 1.0 / total
    weights = [w * inverse for w in weights]
    for h in range(GROUP):
        cols = slice(h * DH, (h + 1) * DH)
        value = None
        for i in range(pairs):
            both = in_ref[i * 16 : (i + 1) * 16, cols].astype(F32)
            term = (
                both[:ROWS] * weights[2 * i][:, h : h + 1]
                + both[ROWS:] * weights[2 * i + 1][:, h : h + 1]
            )
            value = term if value is None else value + term
        twice = jnp.concatenate([value, value], axis=0).astype(BF16)
        for i in range(out_ref.shape[0] // 16):
            out_ref[i * 16 : (i + 1) * 16, cols] = twice


def finish(states):
    return pl.pallas_call(
        finish_kernel,
        out_shape=jax.ShapeDtypeStruct((ZN // 2 * ROWS, WIDE), BF16),
        in_specs=[in_vmem()],
        out_specs=in_vmem(),
        compiler_params=pltpu.CompilerParams(vmem_limit_bytes=VMEM_LIMIT),
    )(states)


def project_kernel(core_ref, a_ref, w0_ref, w1_ref, out_ref):
    core = core_ref[0]
    rows = a_ref[...].reshape(XN * ZN * ROWS, WIDE)
    for side, w_ref in enumerate((w0_ref, w1_ref)):
        result = jnp.dot(rows, w_ref[...], preferred_element_type=F32)
        target = core if side == 0 else 1 - core
        for w in range(ZN):
            pair, low = w // 2, w % 2
            starts = [((low * XN + x) * (ZN // 2) + pair) * ROWS for x in range(XN)]
            chunk = jnp.concatenate([result[start : start + ROWS] for start in starts], axis=0)
            out_ref[target, lax.rem(w + core, ZN)] = chunk.astype(BF16)


def project(core, rows, w0, w1):
    return pl.pallas_call(
        project_kernel,
        out_shape=jax.ShapeDtypeStruct((2, ZN, XN * ROWS, w0.shape[1]), BF16),
        in_specs=[in_smem()] + [in_vmem()] * 3,
        out_specs=in_vmem(),
        compiler_params=pltpu.CompilerParams(vmem_limit_bytes=VMEM_LIMIT),
    )(core, rows, w0, w1)


def find_hits(block_slots, selected, device, head, local_blocks):
    chosen = lax.dynamic_index_in_dim(selected, head, 0, keepdims=False)
    pair = lax.dynamic_slice_in_dim(block_slots, device // 2 * 2 * local_blocks, 2 * local_blocks)
    pair = pair.reshape(2, local_blocks)
    logical = jnp.where(device % 2 == 0, pair, pair[::-1]).reshape(-1)
    hit = jnp.any(chosen[:, None, :] == logical[None, :, None], axis=2).astype(jnp.int32)
    last = (logical == block_slots.shape[0] - 1).astype(jnp.int32)
    return hit * (1 + last[None, :])


def body(queries, keys, values, block_slots, selected, out_weight):
    device = lax.axis_index("ctx")
    head = lax.axis_index("kvh")
    core = (device % 2).reshape(1).astype(jnp.int32)
    where = jnp.stack([device // 2 % XN, device % 2]).astype(jnp.int32)
    hits = find_hits(block_slots, selected, device, head, keys.shape[0] // BLKSZ)
    other_keys = lax.ppermute(keys, "ctx", CORE_SWAP)
    other_values = lax.ppermute(values, "ctx", CORE_SWAP)

    column = spread(queries, "ctx", Z_GROUPS).reshape(ZN * ROWS, WIDE)
    cache = (keys, values, other_keys, other_values)
    own, listed = attend_own(where, column.reshape(NQB, 16, WIDE), hits, cache)
    plane = spread(column, "ctx", X_GROUPS).reshape(XN, NQB, 16, WIDE)
    states = attend_rest(where, plane, listed, cache)
    states, out_weight = lax.optimization_barrier((states, out_weight))
    other_weight = lax.ppermute(out_weight, "ctx", CORE_SWAP)
    merged = merge(where, own, exchange(states, "ctx", X_GROUPS))
    arrived = exchange(merged.reshape(ZN, ROWS, STATE), "ctx", Z_GROUPS)
    attended = finish(arrived.reshape(ZN * ROWS, STATE)).reshape(ZN // 2, ROWS, WIDE)

    column = exchange(attended, "ctx", FAR_GROUPS).reshape(ZN // 2 * ROWS, WIDE)
    plane = spread(column, "ctx", NEAR_GROUPS)
    shares = project(core, plane, out_weight, other_weight)
    arrived = exchange(shares.reshape(2 * YN, XN * ROWS, -1), ("ctx", "kvh"), YC_GROUPS)
    summed = jnp.sum(arrived.reshape(2, YN, XN, ROWS, -1).astype(F32), axis=1)
    return jnp.swapaxes(summed, 0, 1).reshape(XN * 2 * ROWS, -1)


def solution(mesh):
    return jax.shard_map(
        body,
        mesh=mesh,
        in_specs=(P("ctx", "kvh"), P("ctx", "kvh"), P("ctx", "kvh"), P(), P(), P("kvh", "ctx")),
        out_specs=P("kvh", "ctx"),
        check_vma=False,
    )
```

```python
import functools
import math

import jax
import jax.numpy as jnp
from jax import lax
from jax.experimental import pallas as pl
from jax.experimental.pallas import tpu as pltpu
from jax.sharding import PartitionSpec as P

DH = 128
GROUP = 16
BLKSZ = 512
QBLK = 128
NQB = 4
ZN = 8
XN = 4
YN = 8
ROWS = 8
WIDE = GROUP * DH
STATE = WIDE + 128
SCALE = math.log2(math.e) / math.sqrt(DH)
NEG = -(2.0**100)
REST_STEP = 4
OWN_STEP = 4
VMEM_LIMIT = 24 * 1024 * 1024
F32 = jnp.float32
BF16 = jnp.bfloat16


def place(z, x, core):
    return (z * XN + x) * 2 + core


Z_GROUPS = [[place(z, x, c) for z in range(ZN)] for x in range(XN) for c in range(2)]
X_GROUPS = [[place(z, x, c) for x in range(XN)] for z in range(ZN) for c in range(2)]
NEAR_GROUPS = [
    [place((2 * pair + low + c) % ZN, x, c) for low in range(2) for x in range(XN)]
    for pair in range(ZN // 2)
    for c in range(2)
]
FAR_GROUPS = [
    [place((2 * pair + low + c) % ZN, x, c) for pair in range(ZN // 2)]
    for low in range(2)
    for x in range(XN)
    for c in range(2)
]
YC_GROUPS = [
    [place(z, x, c) * YN + y for c in range(2) for y in range(YN)]
    for z in range(ZN)
    for x in range(XN)
]
CORE_SWAP = [(place(z, x, c), place(z, x, 1 - c)) for z in range(ZN) for x in range(XN) for c in range(2)]


def exchange(blocks, axis, groups):
    return lax.all_to_all(
        blocks, axis, split_axis=0, concat_axis=0, tiled=True, axis_index_groups=groups
    )


def spread(rows, axis, groups):
    count = len(groups[0])
    return exchange(jnp.broadcast_to(rows[None], (count,) + rows.shape), axis, groups)


def in_vmem():
    return pl.BlockSpec(memory_space=pltpu.VMEM)


def in_hbm():
    return pl.BlockSpec(memory_space=pltpu.HBM)


def in_smem():
    return pl.BlockSpec(memory_space=pltpu.SMEM)


def attend_kernel(alone, place_ref, q_ref, *rest):
    tile = GROUP * 16
    column = place_ref[0]
    core = place_ref[1]
    if alone:
        hits_ref, k0_ref, v0_ref, k1_ref, v1_ref, final_ref, listed, out_ref = rest[:8]
        parts = [column]
    else:
        listed, k0_ref, v0_ref, k1_ref, v1_ref, out_ref = rest[:6]
        parts = [lax.rem(column + j, XN) for j in range(1, XN)]
    top, total, acc, scaled, k_all, v_all, sems = rest[8 if alone else 6 :]
    local = k0_ref.shape[0]
    blocks = 2 * local // BLKSZ
    found_at = NQB * blocks + 1
    current_at = NQB * blocks + 2
    copies = []
    for i, (source, target, start) in enumerate(
        ((k0_ref, k_all, 0), (v0_ref, v_all, 0), (k1_ref, k_all, local), (v1_ref, v_all, local))
    ):
        copy = pltpu.make_async_copy(source, target.at[pl.ds(start, local)], sems.at[i])
        copy.start()
        copies.append(copy)

    if alone:

        def collect(at, found):
            kind = hits_ref[at // blocks, at % blocks]
            listed[found] = at

            @pl.when(kind == 2)
            def _():
                listed[current_at] = at % blocks

            return found + jnp.where(kind == 1, 1, 0)

        listed[current_at] = -1
        listed[found_at] = lax.fori_loop(0, NQB * blocks, collect, 0)

    def block_of(ref, b):
        return ref[pl.ds(pl.multiple_of(b * BLKSZ, BLKSZ), BLKSZ), :]

    def state_of(ref, c, i):
        return ref.at[c, i * tile : (i + 1) * tile]

    def score(c, i, b):
        kblk = block_of(k_all, b)
        return lax.dot_general(
            state_of(scaled, c, i)[...],
            jnp.concatenate([kblk, kblk], axis=1),
            (((1,), (1,)), ((), ())),
            preferred_element_type=F32,
        )

    def soften(c, i, scores):
        top_ref, total_ref = state_of(top, c, i), state_of(total, c, i)
        old_top = top_ref[...]
        new_top = jnp.maximum(old_top, jnp.max(scores, axis=1, keepdims=True))
        fade = jnp.exp2(old_top - new_top)
        probs = []
        added = None
        for j in range(BLKSZ // 128):
            part = jnp.exp2(scores[:, j * 128 : (j + 1) * 128] - new_top)
            added = part if added is None else added + part
            probs.append(part.astype(BF16))
        top_ref[...] = new_top
        total_ref[...] = total_ref[...] * fade + added
        return jnp.concatenate(probs, axis=1), fade

    def gather(c, i, b, probs, fade):
        acc_ref = state_of(acc, c, i)
        acc_ref[...] = acc_ref[...] * fade + jnp.dot(
            probs, block_of(v_all, b), preferred_element_type=F32
        )

    def run(items, masked=False):
        work = [(c, i, b) for c, b in items for i in range(len(parts))]
        scores = score(*work[0])
        before = None
        for at, (c, i, b) in enumerate(work):
            following = score(*work[at + 1]) if at + 1 < len(work) else None
            if masked:
                row = lax.broadcasted_iota(jnp.int32, (tile, BLKSZ), 0) % 16
                token = (((2 * c + row // 8) * XN + parts[i]) * 2 + core) * ROWS + row % 8
                position = lax.broadcasted_iota(jnp.int32, (tile, BLKSZ), 1)
                scores = jnp.where(position <= token, scores, NEG)
            probs, fade = soften(c, i, scores)
            if before is not None:
                gather(*before)
            before = (c, i, b, probs, fade)
            scores = following
        gather(*before)

    def prepare(c, carry):
        for i, x in enumerate(parts):
            source = q_ref.at[c] if alone else q_ref.at[x, c]
            rows = jnp.concatenate([source[:, h * DH : (h + 1) * DH] for h in range(GROUP)], axis=0)
            rows = rows.astype(F32) * SCALE
            high = rows.astype(BF16)
            low = (rows - high.astype(F32)).astype(BF16)
            state_of(scaled, c, i)[...] = jnp.concatenate([high, low], axis=1)
        return carry

    def item(at):
        return listed[at] // blocks, listed[at] % blocks

    def several(j, carry):
        run([item(step * j + at) for at in range(step)])
        return carry

    def query_block(c, carry):
        first = pl.multiple_of(c * 16, 16)
        lane = lax.broadcasted_iota(jnp.int32, (16, 128), 1)
        for i, x in enumerate(parts):
            target = out_ref if alone else out_ref.at[x]
            peak = state_of(top, c, i)[...]
            kept = peak.astype(BF16).astype(F32)
            factor = jnp.exp2(peak - kept)
            values = (state_of(acc, c, i)[...] * factor).astype(BF16)
            summed = jnp.sum(state_of(total, c, i)[...], axis=1, keepdims=True) * factor
            high = summed.astype(BF16).astype(F32)
            low = summed - high
            stats = jnp.zeros((16, 128), F32)
            for h in range(GROUP):
                rows = slice(h * 16, (h + 1) * 16)
                target[pl.ds(first, 16), h * DH : (h + 1) * DH] = values[rows]
                stats = jnp.where(lane == h, kept[rows], stats)
                stats = jnp.where(lane == GROUP + h, high[rows], stats)
                stats = jnp.where(lane == 2 * GROUP + h, low[rows], stats)
            target[pl.ds(first, 16), WIDE:] = stats.astype(BF16)
        return carry

    top[...] = jnp.full(top.shape, NEG, F32)
    total[...] = jnp.zeros(total.shape, F32)
    acc[...] = jnp.zeros(acc.shape, F32)
    lax.fori_loop(0, NQB, prepare, 0)
    for copy in copies:
        copy.wait()
    found = listed[found_at]
    current = listed[current_at]
    step = OWN_STEP if alone else REST_STEP
    lax.fori_loop(0, found // step, several, 0)
    rest_at = found // step * step

    @pl.when(found - rest_at >= 2)
    def _():
        run([item(rest_at), item(rest_at + 1)])

    @pl.when((found - rest_at) % 2 == 1)
    def _():
        run([item(found - 1)])

    @pl.when(current >= 0)
    def _():
        run([(c, current) for c in range(NQB)], masked=True)

    lax.fori_loop(0, NQB, query_block, 0)
    if alone:
        copy = pltpu.make_async_copy(out_ref, final_ref, sems.at[4])
        copy.start()
        copy.wait()


def state_scratch(parts, tokens):
    tile = parts * GROUP * 16
    return [
        pltpu.VMEM((NQB, tile, 128), F32),
        pltpu.VMEM((NQB, tile, 128), F32),
        pltpu.VMEM((NQB, tile, DH), F32),
        pltpu.VMEM((NQB, tile, 2 * DH), BF16),
        pltpu.VMEM((tokens, DH), BF16),
        pltpu.VMEM((tokens, DH), BF16),
        pltpu.SemaphoreType.DMA((5,)),
    ]


def attend_cost(parts):
    pairs = 8 * parts * GROUP * 16 * BLKSZ
    return pl.CostEstimate(flops=pairs * 4 * DH, bytes_accessed=8 * 1024 * 1024, transcendentals=pairs)


def attend_own(where, q, hits, cache):
    tokens = 2 * cache[0].shape[0]
    state = jax.ShapeDtypeStruct((NQB * 16, STATE), BF16)
    return pl.pallas_call(
        functools.partial(attend_kernel, True),
        name="attend_own",
        out_shape=(state, jax.ShapeDtypeStruct((NQB * tokens // BLKSZ + 8,), jnp.int32)),
        in_specs=[in_smem(), in_vmem(), in_smem()] + [in_hbm()] * 4,
        out_specs=(in_hbm(), in_smem()),
        scratch_shapes=[pltpu.VMEM(state.shape, BF16)] + state_scratch(1, tokens),
        compiler_params=pltpu.CompilerParams(vmem_limit_bytes=VMEM_LIMIT),
        cost_estimate=attend_cost(1),
    )(where, q, hits, *cache)


def attend_rest(where, q, listed, cache):
    return pl.pallas_call(
        functools.partial(attend_kernel, False),
        name="attend_rest",
        out_shape=jax.ShapeDtypeStruct((XN, NQB * 16, STATE), BF16),
        in_specs=[in_smem(), in_vmem(), in_smem()] + [in_hbm()] * 4,
        out_specs=in_vmem(),
        scratch_shapes=state_scratch(XN - 1, 2 * cache[0].shape[0]),
        compiler_params=pltpu.CompilerParams(vmem_limit_bytes=VMEM_LIMIT),
        cost_estimate=attend_cost(XN - 1),
    )(where, q, listed, *cache)


def weights_of(stats):
    tops = [s[:, :GROUP] for s in stats]
    peak = tops[0]
    for t in tops[1:]:
        peak = jnp.maximum(peak, t)
    weights = [jnp.exp2(t - peak) for t in tops]
    total = None
    for w, s in zip(weights, stats):
        term = w * (s[:, GROUP : 2 * GROUP] + s[:, 2 * GROUP : 3 * GROUP])
        total = term if total is None else total + term
    return peak, weights, total


def merge_kernel(place_ref, own_ref, in_ref, out_ref):
    rows = own_ref.shape[0]
    column = place_ref[0]
    sources = [own_ref] + [in_ref.at[lax.rem(column + j, XN)] for j in range(1, XN)]
    peak, weights, total = weights_of([s[:, WIDE:].astype(F32) for s in sources])
    for h in range(GROUP):
        cols = slice(h * DH, (h + 1) * DH)
        value = None
        for source, weight in zip(sources, weights):
            term = source[:, cols].astype(F32) * weight[:, h : h + 1]
            value = term if value is None else value + term
        out_ref[:, cols] = value.astype(BF16)
    high = total.astype(BF16).astype(F32)
    rest = jnp.zeros((rows, 128 - 3 * GROUP), F32)
    out_ref[:, WIDE:] = jnp.concatenate([peak, high, total - high, rest], axis=1).astype(BF16)


def merge(where, own, states):
    return pl.pallas_call(
        merge_kernel,
        name="merge",
        out_shape=jax.ShapeDtypeStruct(states.shape[1:], BF16),
        in_specs=[in_smem(), in_vmem(), in_vmem()],
        out_specs=in_vmem(),
        compiler_params=pltpu.CompilerParams(vmem_limit_bytes=VMEM_LIMIT),
    )(where, own, states)


def finish_kernel(in_ref, out_ref):
    pairs = in_ref.shape[0] // 16
    stats = []
    for i in range(pairs):
        both = in_ref[i * 16 : (i + 1) * 16, WIDE:].astype(F32)
        stats += [both[:ROWS], both[ROWS:]]
    _, weights, total = weights_of(stats)
    inverse = 1.0 / total
    weights = [w * inverse for w in weights]
    for h in range(GROUP):
        cols = slice(h * DH, (h + 1) * DH)
        value = None
        for i in range(pairs):
            both = in_ref[i * 16 : (i + 1) * 16, cols].astype(F32)
            term = (
                both[:ROWS] * weights[2 * i][:, h : h + 1]
                + both[ROWS:] * weights[2 * i + 1][:, h : h + 1]
            )
            value = term if value is None else value + term
        twice = jnp.concatenate([value, value], axis=0).astype(BF16)
        for i in range(out_ref.shape[0] // 16):
            out_ref[i * 16 : (i + 1) * 16, cols] = twice


def finish(states):
    return pl.pallas_call(
        finish_kernel,
        out_shape=jax.ShapeDtypeStruct((ZN // 2 * ROWS, WIDE), BF16),
        in_specs=[in_vmem()],
        out_specs=in_vmem(),
        compiler_params=pltpu.CompilerParams(vmem_limit_bytes=VMEM_LIMIT),
    )(states)


def project_kernel(core_ref, a_ref, w0_ref, w1_ref, out_ref):
    core = core_ref[0]
    rows = a_ref[...].reshape(XN * ZN * ROWS, WIDE)
    for side, w_ref in enumerate((w0_ref, w1_ref)):
        result = jnp.dot(rows, w_ref[...], preferred_element_type=F32)
        target = core if side == 0 else 1 - core
        for w in range(ZN):
            pair, low = w // 2, w % 2
            starts = [((low * XN + x) * (ZN // 2) + pair) * ROWS for x in range(XN)]
            chunk = jnp.concatenate([result[start : start + ROWS] for start in starts], axis=0)
            out_ref[target, lax.rem(w + core, ZN)] = chunk.astype(BF16)


def project(core, rows, w0, w1):
    return pl.pallas_call(
        project_kernel,
        out_shape=jax.ShapeDtypeStruct((2, ZN, XN * ROWS, w0.shape[1]), BF16),
        in_specs=[in_smem()] + [in_vmem()] * 3,
        out_specs=in_vmem(),
        compiler_params=pltpu.CompilerParams(vmem_limit_bytes=VMEM_LIMIT),
    )(core, rows, w0, w1)


def find_hits(block_slots, selected, device, head, local_blocks):
    chosen = lax.dynamic_index_in_dim(selected, head, 0, keepdims=False)
    pair = lax.dynamic_slice_in_dim(block_slots, device // 2 * 2 * local_blocks, 2 * local_blocks)
    pair = pair.reshape(2, local_blocks)
    logical = jnp.where(device % 2 == 0, pair, pair[::-1]).reshape(-1)
    hit = jnp.any(chosen[:, None, :] == logical[None, :, None], axis=2).astype(jnp.int32)
    last = (logical == block_slots.shape[0] - 1).astype(jnp.int32)
    return hit * (1 + last[None, :])


def body(queries, keys, values, block_slots, selected, out_weight):
    device = lax.axis_index("ctx")
    head = lax.axis_index("kvh")
    core = (device % 2).reshape(1).astype(jnp.int32)
    where = jnp.stack([device // 2 % XN, device % 2]).astype(jnp.int32)
    hits = find_hits(block_slots, selected, device, head, keys.shape[0] // BLKSZ)
    other_keys = lax.ppermute(keys, "ctx", CORE_SWAP)
    other_values = lax.ppermute(values, "ctx", CORE_SWAP)

    column = spread(queries, "ctx", Z_GROUPS).reshape(ZN * ROWS, WIDE)
    cache = (keys, values, other_keys, other_values)
    own, listed = attend_own(where, column.reshape(NQB, 16, WIDE), hits, cache)
    plane = spread(column, "ctx", X_GROUPS).reshape(XN, NQB, 16, WIDE)
    states = attend_rest(where, plane, listed, cache)
    states, out_weight = lax.optimization_barrier((states, out_weight))
    other_weight = lax.ppermute(out_weight, "ctx", CORE_SWAP)
    merged = merge(where, own, exchange(states, "ctx", X_GROUPS))
    arrived = exchange(merged.reshape(ZN, ROWS, STATE), "ctx", Z_GROUPS)
    attended = finish(arrived.reshape(ZN * ROWS, STATE)).reshape(ZN // 2, ROWS, WIDE)

    column = exchange(attended, "ctx", FAR_GROUPS).reshape(ZN // 2 * ROWS, WIDE)
    plane = spread(column, "ctx", NEAR_GROUPS)
    shares = project(core, plane, out_weight, other_weight)
    arrived = exchange(shares.reshape(2 * YN, XN * ROWS, -1), ("ctx", "kvh"), YC_GROUPS)
    summed = jnp.sum(arrived.reshape(2, YN, XN, ROWS, -1).astype(F32), axis=1)
    return jnp.swapaxes(summed, 0, 1).reshape(XN * 2 * ROWS, -1)


def solution(mesh):
    return jax.shard_map(
        body,
        mesh=mesh,
        in_specs=(P("ctx", "kvh"), P("ctx", "kvh"), P("ctx", "kvh"), P(), P(), P("kvh", "ctx")),
        out_specs=P("kvh", "ctx"),
        check_vma=False,
    )
```

```python
import functools
import math

import jax
import jax.numpy as jnp
from jax import lax
from jax.experimental import pallas as pl
from jax.experimental.pallas import tpu as pltpu
from jax.sharding import PartitionSpec as P

DH = 128
GROUP = 16
BLKSZ = 512
QBLK = 128
NQB = 4
ZN = 8
XN = 4
YN = 8
ROWS = 8
WIDE = GROUP * DH
STATE = WIDE + 128
SCALE = math.log2(math.e) / math.sqrt(DH)
NEG = -(2.0**100)
REST_STEP = 4
OWN_STEP = 4
VMEM_LIMIT = 24 * 1024 * 1024
F32 = jnp.float32
BF16 = jnp.bfloat16


def place(z, x, core):
    return (z * XN + x) * 2 + core


Z_GROUPS = [[place(z, x, c) for z in range(ZN)] for x in range(XN) for c in range(2)]
X_GROUPS = [[place(z, x, c) for x in range(XN)] for z in range(ZN) for c in range(2)]
NEAR_GROUPS = [
    [place((2 * pair + low + c) % ZN, x, c) for low in range(2) for x in range(XN)]
    for pair in range(ZN // 2)
    for c in range(2)
]
FAR_GROUPS = [
    [place((2 * pair + low + c) % ZN, x, c) for pair in range(ZN // 2)]
    for low in range(2)
    for x in range(XN)
    for c in range(2)
]
YC_GROUPS = [
    [place(z, x, c) * YN + y for c in range(2) for y in range(YN)]
    for z in range(ZN)
    for x in range(XN)
]
CORE_SWAP = [(place(z, x, c), place(z, x, 1 - c)) for z in range(ZN) for x in range(XN) for c in range(2)]


def exchange(blocks, axis, groups):
    return lax.all_to_all(
        blocks, axis, split_axis=0, concat_axis=0, tiled=True, axis_index_groups=groups
    )


def spread(rows, axis, groups):
    count = len(groups[0])
    return exchange(jnp.broadcast_to(rows[None], (count,) + rows.shape), axis, groups)


def in_vmem():
    return pl.BlockSpec(memory_space=pltpu.VMEM)


def in_hbm():
    return pl.BlockSpec(memory_space=pltpu.HBM)


def in_smem():
    return pl.BlockSpec(memory_space=pltpu.SMEM)


def attend_kernel(alone, place_ref, q_ref, *rest):
    tile = GROUP * 16
    column = place_ref[0]
    core = place_ref[1]
    if alone:
        hits_ref, k0_ref, v0_ref, k1_ref, v1_ref, final_ref, listed, out_ref = rest[:8]
        parts = [column]
    else:
        listed, k0_ref, v0_ref, k1_ref, v1_ref, final_ref, out_ref = rest[:7]
        parts = [lax.rem(column + j, XN) for j in range(1, XN)]
    top, total, acc, scaled, k_all, v_all, sems = rest[8 if alone else 7 :]
    local = k0_ref.shape[0]
    blocks = 2 * local // BLKSZ
    found_at = NQB * blocks + 1
    current_at = NQB * blocks + 2
    copies = []
    for i, (source, target, start) in enumerate(
        ((k0_ref, k_all, 0), (v0_ref, v_all, 0), (k1_ref, k_all, local), (v1_ref, v_all, local))
    ):
        copy = pltpu.make_async_copy(source, target.at[pl.ds(start, local)], sems.at[i])
        copy.start()
        copies.append(copy)

    if alone:

        def collect(at, found):
            kind = hits_ref[at // blocks, at % blocks]
            listed[found] = at

            @pl.when(kind == 2)
            def _():
                listed[current_at] = at % blocks

            return found + jnp.where(kind == 1, 1, 0)

        listed[current_at] = -1
        listed[found_at] = lax.fori_loop(0, NQB * blocks, collect, 0)

    def block_of(ref, b):
        return ref[pl.ds(pl.multiple_of(b * BLKSZ, BLKSZ), BLKSZ), :]

    def state_of(ref, c, i):
        return ref.at[c, i * tile : (i + 1) * tile]

    def score(c, i, b):
        kblk = block_of(k_all, b)
        return lax.dot_general(
            state_of(scaled, c, i)[...],
            jnp.concatenate([kblk, kblk], axis=1),
            (((1,), (1,)), ((), ())),
            preferred_element_type=F32,
        )

    def soften(c, i, scores):
        top_ref, total_ref = state_of(top, c, i), state_of(total, c, i)
        old_top = top_ref[...]
        new_top = jnp.maximum(old_top, jnp.max(scores, axis=1, keepdims=True))
        fade = jnp.exp2(old_top - new_top)
        probs = []
        added = None
        for j in range(BLKSZ // 128):
            part = jnp.exp2(scores[:, j * 128 : (j + 1) * 128] - new_top)
            added = part if added is None else added + part
            probs.append(part.astype(BF16))
        top_ref[...] = new_top
        total_ref[...] = total_ref[...] * fade + added
        return jnp.concatenate(probs, axis=1), fade

    def gather(c, i, b, probs, fade):
        acc_ref = state_of(acc, c, i)
        acc_ref[...] = acc_ref[...] * fade + jnp.dot(
            probs, block_of(v_all, b), preferred_element_type=F32
        )

    def run(items, masked=False):
        work = [(c, i, b) for c, b in items for i in range(len(parts))]
        scores = score(*work[0])
        before = None
        for at, (c, i, b) in enumerate(work):
            following = score(*work[at + 1]) if at + 1 < len(work) else None
            if masked:
                row = lax.broadcasted_iota(jnp.int32, (tile, BLKSZ), 0) % 16
                token = (((2 * c + row // 8) * XN + parts[i]) * 2 + core) * ROWS + row % 8
                position = lax.broadcasted_iota(jnp.int32, (tile, BLKSZ), 1)
                scores = jnp.where(position <= token, scores, NEG)
            probs, fade = soften(c, i, scores)
            if before is not None:
                gather(*before)
            before = (c, i, b, probs, fade)
            scores = following
        gather(*before)

    def prepare(c, carry):
        for i, x in enumerate(parts):
            source = q_ref.at[c] if alone else q_ref.at[x, c]
            rows = jnp.concatenate([source[:, h * DH : (h + 1) * DH] for h in range(GROUP)], axis=0)
            rows = rows.astype(F32) * SCALE
            high = rows.astype(BF16)
            low = (rows - high.astype(F32)).astype(BF16)
            state_of(scaled, c, i)[...] = jnp.concatenate([high, low], axis=1)
        return carry

    def item(at):
        return listed[at] // blocks, listed[at] % blocks

    def several(j, carry):
        run([item(step * j + at) for at in range(step)])
        return carry

    def leave(c, i):
        rows = pl.ds(pl.multiple_of(c * 16, 16), 16)
        return pltpu.make_async_copy(
            out_ref.at[parts[i], rows], final_ref.at[parts[i], rows], sems.at[4 + c * len(parts) + i]
        )

    def query_block(c, carry):
        first = pl.multiple_of(c * 16, 16)
        lane = lax.broadcasted_iota(jnp.int32, (16, 128), 1)
        for i, x in enumerate(parts):
            target = out_ref if alone else out_ref.at[x]
            peak = state_of(top, c, i)[...]
            kept = peak.astype(BF16).astype(F32)
            factor = jnp.exp2(peak - kept)
            values = (state_of(acc, c, i)[...] * factor).astype(BF16)
            summed = jnp.sum(state_of(total, c, i)[...], axis=1, keepdims=True) * factor
            high = summed.astype(BF16).astype(F32)
            low = summed - high
            stats = jnp.zeros((16, 128), F32)
            for h in range(GROUP):
                rows = slice(h * 16, (h + 1) * 16)
                target[pl.ds(first, 16), h * DH : (h + 1) * DH] = values[rows]
                stats = jnp.where(lane == h, kept[rows], stats)
                stats = jnp.where(lane == GROUP + h, high[rows], stats)
                stats = jnp.where(lane == 2 * GROUP + h, low[rows], stats)
            target[pl.ds(first, 16), WIDE:] = stats.astype(BF16)
            if not alone:
                leave(c, i).start()
        return carry

    top[...] = jnp.full(top.shape, NEG, F32)
    total[...] = jnp.zeros(total.shape, F32)
    acc[...] = jnp.zeros(acc.shape, F32)
    lax.fori_loop(0, NQB, prepare, 0)
    for copy in copies:
        copy.wait()
    found = listed[found_at]
    current = listed[current_at]
    step = OWN_STEP if alone else REST_STEP
    lax.fori_loop(0, found // step, several, 0)
    rest_at = found // step * step

    @pl.when(found - rest_at >= 2)
    def _():
        run([item(rest_at), item(rest_at + 1)])

    @pl.when((found - rest_at) % 2 == 1)
    def _():
        run([item(found - 1)])

    @pl.when(current >= 0)
    def _():
        run([(c, current) for c in range(NQB)], masked=True)

    lax.fori_loop(0, NQB, query_block, 0)
    if not alone:
        for c in range(NQB):
            for i in range(len(parts)):
                leave(c, i).wait()
    if alone:
        copy = pltpu.make_async_copy(out_ref, final_ref, sems.at[4])
        copy.start()
        copy.wait()


def state_scratch(parts, tokens):
    tile = parts * GROUP * 16
    return [
        pltpu.VMEM((NQB, tile, 128), F32),
        pltpu.VMEM((NQB, tile, 128), F32),
        pltpu.VMEM((NQB, tile, DH), F32),
        pltpu.VMEM((NQB, tile, 2 * DH), BF16),
        pltpu.VMEM((tokens, DH), BF16),
        pltpu.VMEM((tokens, DH), BF16),
        pltpu.SemaphoreType.DMA((4 + NQB * parts,)),
    ]


def attend_cost(parts):
    pairs = 8 * parts * GROUP * 16 * BLKSZ
    return pl.CostEstimate(flops=pairs * 4 * DH, bytes_accessed=8 * 1024 * 1024, transcendentals=pairs)


def attend_own(where, q, hits, cache):
    tokens = 2 * cache[0].shape[0]
    state = jax.ShapeDtypeStruct((NQB * 16, STATE), BF16)
    return pl.pallas_call(
        functools.partial(attend_kernel, True),
        name="attend_own",
        out_shape=(state, jax.ShapeDtypeStruct((NQB * tokens // BLKSZ + 8,), jnp.int32)),
        in_specs=[in_smem(), in_vmem(), in_smem()] + [in_hbm()] * 4,
        out_specs=(in_hbm(), in_smem()),
        scratch_shapes=[pltpu.VMEM(state.shape, BF16)] + state_scratch(1, tokens),
        compiler_params=pltpu.CompilerParams(vmem_limit_bytes=VMEM_LIMIT),
        cost_estimate=attend_cost(1),
    )(where, q, hits, *cache)


def attend_rest(where, q, listed, cache):
    states = jax.ShapeDtypeStruct((XN, NQB * 16, STATE), BF16)
    return pl.pallas_call(
        functools.partial(attend_kernel, False),
        name="attend_rest",
        out_shape=states,
        in_specs=[in_smem(), in_vmem(), in_smem()] + [in_hbm()] * 4,
        out_specs=in_hbm(),
        scratch_shapes=[pltpu.VMEM(states.shape, BF16)] + state_scratch(XN - 1, 2 * cache[0].shape[0]),
        compiler_params=pltpu.CompilerParams(vmem_limit_bytes=VMEM_LIMIT),
        cost_estimate=attend_cost(XN - 1),
    )(where, q, listed, *cache)


def weights_of(stats):
    tops = [s[:, :GROUP] for s in stats]
    peak = tops[0]
    for t in tops[1:]:
        peak = jnp.maximum(peak, t)
    weights = [jnp.exp2(t - peak) for t in tops]
    total = None
    for w, s in zip(weights, stats):
        term = w * (s[:, GROUP : 2 * GROUP] + s[:, 2 * GROUP : 3 * GROUP])
        total = term if total is None else total + term
    return peak, weights, total


def merge_kernel(place_ref, own_ref, in_ref, out_ref):
    rows = own_ref.shape[0]
    column = place_ref[0]
    sources = [own_ref] + [in_ref.at[lax.rem(column + j, XN)] for j in range(1, XN)]
    peak, weights, total = weights_of([s[:, WIDE:].astype(F32) for s in sources])
    for h in range(GROUP):
        cols = slice(h * DH, (h + 1) * DH)
        value = None
        for source, weight in zip(sources, weights):
            term = source[:, cols].astype(F32) * weight[:, h : h + 1]
            value = term if value is None else value + term
        out_ref[:, cols] = value.astype(BF16)
    high = total.astype(BF16).astype(F32)
    rest = jnp.zeros((rows, 128 - 3 * GROUP), F32)
    out_ref[:, WIDE:] = jnp.concatenate([peak, high, total - high, rest], axis=1).astype(BF16)


def merge(where, own, states):
    return pl.pallas_call(
        merge_kernel,
        name="merge",
        out_shape=jax.ShapeDtypeStruct(states.shape[1:], BF16),
        in_specs=[in_smem(), in_vmem(), in_vmem()],
        out_specs=in_vmem(),
        compiler_params=pltpu.CompilerParams(vmem_limit_bytes=VMEM_LIMIT),
    )(where, own, states)


def finish_kernel(in_ref, out_ref):
    pairs = in_ref.shape[0] // 16
    stats = []
    for i in range(pairs):
        both = in_ref[i * 16 : (i + 1) * 16, WIDE:].astype(F32)
        stats += [both[:ROWS], both[ROWS:]]
    _, weights, total = weights_of(stats)
    inverse = 1.0 / total
    weights = [w * inverse for w in weights]
    for h in range(GROUP):
        cols = slice(h * DH, (h + 1) * DH)
        value = None
        for i in range(pairs):
            both = in_ref[i * 16 : (i + 1) * 16, cols].astype(F32)
            term = (
                both[:ROWS] * weights[2 * i][:, h : h + 1]
                + both[ROWS:] * weights[2 * i + 1][:, h : h + 1]
            )
            value = term if value is None else value + term
        twice = jnp.concatenate([value, value], axis=0).astype(BF16)
        for i in range(out_ref.shape[0] // 16):
            out_ref[i * 16 : (i + 1) * 16, cols] = twice


def finish(states):
    return pl.pallas_call(
        finish_kernel,
        out_shape=jax.ShapeDtypeStruct((ZN // 2 * ROWS, WIDE), BF16),
        in_specs=[in_vmem()],
        out_specs=in_vmem(),
        compiler_params=pltpu.CompilerParams(vmem_limit_bytes=VMEM_LIMIT),
    )(states)


def project_kernel(core_ref, a_ref, w0_ref, w1_ref, out_ref):
    core = core_ref[0]
    rows = a_ref[...].reshape(XN * ZN * ROWS, WIDE)
    for side, w_ref in enumerate((w0_ref, w1_ref)):
        result = jnp.dot(rows, w_ref[...], preferred_element_type=F32)
        target = core if side == 0 else 1 - core
        for w in range(ZN):
            pair, low = w // 2, w % 2
            starts = [((low * XN + x) * (ZN // 2) + pair) * ROWS for x in range(XN)]
            chunk = jnp.concatenate([result[start : start + ROWS] for start in starts], axis=0)
            out_ref[target, lax.rem(w + core, ZN)] = chunk.astype(BF16)


def project(core, rows, w0, w1):
    return pl.pallas_call(
        project_kernel,
        out_shape=jax.ShapeDtypeStruct((2, ZN, XN * ROWS, w0.shape[1]), BF16),
        in_specs=[in_smem()] + [in_vmem()] * 3,
        out_specs=in_vmem(),
        compiler_params=pltpu.CompilerParams(vmem_limit_bytes=VMEM_LIMIT),
    )(core, rows, w0, w1)


def find_hits(block_slots, selected, device, head, local_blocks):
    chosen = lax.dynamic_index_in_dim(selected, head, 0, keepdims=False)
    pair = lax.dynamic_slice_in_dim(block_slots, device // 2 * 2 * local_blocks, 2 * local_blocks)
    pair = pair.reshape(2, local_blocks)
    logical = jnp.where(device % 2 == 0, pair, pair[::-1]).reshape(-1)
    hit = jnp.any(chosen[:, None, :] == logical[None, :, None], axis=2).astype(jnp.int32)
    last = (logical == block_slots.shape[0] - 1).astype(jnp.int32)
    return hit * (1 + last[None, :])


def body(queries, keys, values, block_slots, selected, out_weight):
    device = lax.axis_index("ctx")
    head = lax.axis_index("kvh")
    core = (device % 2).reshape(1).astype(jnp.int32)
    where = jnp.stack([device // 2 % XN, device % 2]).astype(jnp.int32)
    hits = find_hits(block_slots, selected, device, head, keys.shape[0] // BLKSZ)
    other_keys = lax.ppermute(keys, "ctx", CORE_SWAP)
    other_values = lax.ppermute(values, "ctx", CORE_SWAP)

    column = spread(queries, "ctx", Z_GROUPS).reshape(ZN * ROWS, WIDE)
    cache = (keys, values, other_keys, other_values)
    own, listed = attend_own(where, column.reshape(NQB, 16, WIDE), hits, cache)
    plane = spread(column, "ctx", X_GROUPS).reshape(XN, NQB, 16, WIDE)
    states = attend_rest(where, plane, listed, cache)
    states, out_weight = lax.optimization_barrier((states, out_weight))
    other_weight = lax.ppermute(out_weight, "ctx", CORE_SWAP)
    merged = merge(where, own, exchange(states, "ctx", X_GROUPS))
    arrived = exchange(merged.reshape(ZN, ROWS, STATE), "ctx", Z_GROUPS)
    attended = finish(arrived.reshape(ZN * ROWS, STATE)).reshape(ZN // 2, ROWS, WIDE)

    column = exchange(attended, "ctx", FAR_GROUPS).reshape(ZN // 2 * ROWS, WIDE)
    plane = spread(column, "ctx", NEAR_GROUPS)
    shares = project(core, plane, out_weight, other_weight)
    arrived = exchange(shares.reshape(2 * YN, XN * ROWS, -1), ("ctx", "kvh"), YC_GROUPS)
    summed = jnp.sum(arrived.reshape(2, YN, XN, ROWS, -1).astype(F32), axis=1)
    return jnp.swapaxes(summed, 0, 1).reshape(XN * 2 * ROWS, -1)


def solution(mesh):
    return jax.shard_map(
        body,
        mesh=mesh,
        in_specs=(P("ctx", "kvh"), P("ctx", "kvh"), P("ctx", "kvh"), P(), P(), P("kvh", "ctx")),
        out_specs=P("kvh", "ctx"),
        check_vma=False,
    )
```

```python
import functools
import math

import jax
import jax.numpy as jnp
from jax import lax
from jax.experimental import pallas as pl
from jax.experimental.pallas import tpu as pltpu
from jax.sharding import PartitionSpec as P

DH = 128
GROUP = 16
BLKSZ = 512
QBLK = 128
NQB = 4
ZN = 8
XN = 4
YN = 8
ROWS = 8
WIDE = GROUP * DH
STATE = WIDE + 128
SCALE = math.log2(math.e) / math.sqrt(DH)
NEG = -(2.0**100)
REST_STEP = 4
OWN_STEP = 4
VMEM_LIMIT = 24 * 1024 * 1024
F32 = jnp.float32
BF16 = jnp.bfloat16


def place(z, x, core):
    return (z * XN + x) * 2 + core


Z_GROUPS = [[place(z, x, c) for z in range(ZN)] for x in range(XN) for c in range(2)]
X_GROUPS = [[place(z, x, c) for x in range(XN)] for z in range(ZN) for c in range(2)]
NEAR_GROUPS = [
    [place((2 * pair + low + c) % ZN, x, c) for low in range(2) for x in range(XN)]
    for pair in range(ZN // 2)
    for c in range(2)
]
FAR_GROUPS = [
    [place((2 * pair + low + c) % ZN, x, c) for pair in range(ZN // 2)]
    for low in range(2)
    for x in range(XN)
    for c in range(2)
]
YC_GROUPS = [
    [place(z, x, c) * YN + (y + c * (YN // 2)) % YN for c in range(2) for y in range(YN)]
    for z in range(ZN)
    for x in range(XN)
]
CORE_SWAP = [(place(z, x, c), place(z, x, 1 - c)) for z in range(ZN) for x in range(XN) for c in range(2)]


def exchange(blocks, axis, groups):
    return lax.all_to_all(
        blocks, axis, split_axis=0, concat_axis=0, tiled=True, axis_index_groups=groups
    )


def spread(rows, axis, groups):
    count = len(groups[0])
    return exchange(jnp.broadcast_to(rows[None], (count,) + rows.shape), axis, groups)


def in_vmem():
    return pl.BlockSpec(memory_space=pltpu.VMEM)


def in_hbm():
    return pl.BlockSpec(memory_space=pltpu.HBM)


def in_smem():
    return pl.BlockSpec(memory_space=pltpu.SMEM)


def attend_kernel(alone, place_ref, q_ref, *rest):
    tile = GROUP * 16
    column = place_ref[0]
    core = place_ref[1]
    if alone:
        hits_ref, k0_ref, v0_ref, k1_ref, v1_ref, final_ref, listed, out_ref = rest[:8]
        parts = [column]
    else:
        listed, k0_ref, v0_ref, k1_ref, v1_ref, out_ref = rest[:6]
        parts = [lax.rem(column + j, XN) for j in range(1, XN)]
    top, total, acc, scaled, k_all, v_all, sems = rest[8 if alone else 6 :]
    local = k0_ref.shape[0]
    blocks = 2 * local // BLKSZ
    found_at = NQB * blocks + 1
    current_at = NQB * blocks + 2
    copies = []
    for i, (source, target, start) in enumerate(
        ((k0_ref, k_all, 0), (v0_ref, v_all, 0), (k1_ref, k_all, local), (v1_ref, v_all, local))
    ):
        copy = pltpu.make_async_copy(source, target.at[pl.ds(start, local)], sems.at[i])
        copy.start()
        copies.append(copy)

    if alone:

        def collect(at, found):
            kind = hits_ref[at // blocks, at % blocks]
            listed[found] = at

            @pl.when(kind == 2)
            def _():
                listed[current_at] = at % blocks

            return found + jnp.where(kind == 1, 1, 0)

        listed[current_at] = -1
        listed[found_at] = lax.fori_loop(0, NQB * blocks, collect, 0)

    def block_of(ref, b):
        return ref[pl.ds(pl.multiple_of(b * BLKSZ, BLKSZ), BLKSZ), :]

    def state_of(ref, c, i):
        return ref.at[c, i * tile : (i + 1) * tile]

    def score(c, i, b):
        kblk = block_of(k_all, b)
        return lax.dot_general(
            state_of(scaled, c, i)[...],
            jnp.concatenate([kblk, kblk], axis=1),
            (((1,), (1,)), ((), ())),
            preferred_element_type=F32,
        )

    def soften(c, i, scores):
        top_ref, total_ref = state_of(top, c, i), state_of(total, c, i)
        old_top = top_ref[...]
        new_top = jnp.maximum(old_top, jnp.max(scores, axis=1, keepdims=True))
        fade = jnp.exp2(old_top - new_top)
        probs = []
        added = None
        for j in range(BLKSZ // 128):
            part = jnp.exp2(scores[:, j * 128 : (j + 1) * 128] - new_top)
            added = part if added is None else added + part
            probs.append(part.astype(BF16))
        top_ref[...] = new_top
        total_ref[...] = total_ref[...] * fade + added
        return jnp.concatenate(probs, axis=1), fade

    def gather(c, i, b, probs, fade):
        acc_ref = state_of(acc, c, i)
        acc_ref[...] = acc_ref[...] * fade + jnp.dot(
            probs, block_of(v_all, b), preferred_element_type=F32
        )

    def run(items, masked=False):
        work = [(c, i, b) for c, b in items for i in range(len(parts))]
        scores = score(*work[0])
        before = None
        for at, (c, i, b) in enumerate(work):
            following = score(*work[at + 1]) if at + 1 < len(work) else None
            if masked:
                row = lax.broadcasted_iota(jnp.int32, (tile, BLKSZ), 0) % 16
                token = (((2 * c + row // 8) * XN + parts[i]) * 2 + core) * ROWS + row % 8
                position = lax.broadcasted_iota(jnp.int32, (tile, BLKSZ), 1)
                scores = jnp.where(position <= token, scores, NEG)
            probs, fade = soften(c, i, scores)
            if before is not None:
                gather(*before)
            before = (c, i, b, probs, fade)
            scores = following
        gather(*before)

    def prepare(c, carry):
        for i, x in enumerate(parts):
            source = q_ref.at[c] if alone else q_ref.at[x, c]
            rows = jnp.concatenate([source[:, h * DH : (h + 1) * DH] for h in range(GROUP)], axis=0)
            rows = rows.astype(F32) * SCALE
            high = rows.astype(BF16)
            low = (rows - high.astype(F32)).astype(BF16)
            state_of(scaled, c, i)[...] = jnp.concatenate([high, low], axis=1)
        return carry

    def item(at):
        return listed[at] // blocks, listed[at] % blocks

    def several(j, carry):
        run([item(step * j + at) for at in range(step)])
        return carry

    def query_block(c, carry):
        first = pl.multiple_of(c * 16, 16)
        lane = lax.broadcasted_iota(jnp.int32, (16, 128), 1)
        for i, x in enumerate(parts):
            target = out_ref if alone else out_ref.at[x]
            peak = state_of(top, c, i)[...]
            kept = peak.astype(BF16).astype(F32)
            factor = jnp.exp2(peak - kept)
            values = (state_of(acc, c, i)[...] * factor).astype(BF16)
            summed = jnp.sum(state_of(total, c, i)[...], axis=1, keepdims=True) * factor
            high = summed.astype(BF16).astype(F32)
            low = summed - high
            stats = jnp.zeros((16, 128), F32)
            for h in range(GROUP):
                rows = slice(h * 16, (h + 1) * 16)
                target[pl.ds(first, 16), h * DH : (h + 1) * DH] = values[rows]
                stats = jnp.where(lane == h, kept[rows], stats)
                stats = jnp.where(lane == GROUP + h, high[rows], stats)
                stats = jnp.where(lane == 2 * GROUP + h, low[rows], stats)
            target[pl.ds(first, 16), WIDE:] = stats.astype(BF16)
        return carry

    top[...] = jnp.full(top.shape, NEG, F32)
    total[...] = jnp.zeros(total.shape, F32)
    acc[...] = jnp.zeros(acc.shape, F32)
    lax.fori_loop(0, NQB, prepare, 0)
    for copy in copies:
        copy.wait()
    found = listed[found_at]
    current = listed[current_at]
    step = OWN_STEP if alone else REST_STEP
    lax.fori_loop(0, found // step, several, 0)
    rest_at = found // step * step

    @pl.when(found - rest_at >= 2)
    def _():
        run([item(rest_at), item(rest_at + 1)])

    @pl.when((found - rest_at) % 2 == 1)
    def _():
        run([item(found - 1)])

    @pl.when(current >= 0)
    def _():
        run([(c, current) for c in range(NQB)], masked=True)

    lax.fori_loop(0, NQB, query_block, 0)
    if alone:
        copy = pltpu.make_async_copy(out_ref, final_ref, sems.at[4])
        copy.start()
        copy.wait()


def state_scratch(parts, tokens):
    tile = parts * GROUP * 16
    return [
        pltpu.VMEM((NQB, tile, 128), F32),
        pltpu.VMEM((NQB, tile, 128), F32),
        pltpu.VMEM((NQB, tile, DH), F32),
        pltpu.VMEM((NQB, tile, 2 * DH), BF16),
        pltpu.VMEM((tokens, DH), BF16),
        pltpu.VMEM((tokens, DH), BF16),
        pltpu.SemaphoreType.DMA((5,)),
    ]


def attend_cost(parts):
    pairs = 8 * parts * GROUP * 16 * BLKSZ
    return pl.CostEstimate(flops=pairs * 4 * DH, bytes_accessed=8 * 1024 * 1024, transcendentals=pairs)


def attend_own(where, q, hits, cache):
    tokens = 2 * cache[0].shape[0]
    state = jax.ShapeDtypeStruct((NQB * 16, STATE), BF16)
    return pl.pallas_call(
        functools.partial(attend_kernel, True),
        name="attend_own",
        out_shape=(state, jax.ShapeDtypeStruct((NQB * tokens // BLKSZ + 8,), jnp.int32)),
        in_specs=[in_smem(), in_vmem(), in_smem()] + [in_hbm()] * 4,
        out_specs=(in_hbm(), in_smem()),
        scratch_shapes=[pltpu.VMEM(state.shape, BF16)] + state_scratch(1, tokens),
        compiler_params=pltpu.CompilerParams(vmem_limit_bytes=VMEM_LIMIT),
        cost_estimate=attend_cost(1),
    )(where, q, hits, *cache)


def attend_rest(where, q, listed, cache):
    return pl.pallas_call(
        functools.partial(attend_kernel, False),
        name="attend_rest",
        out_shape=jax.ShapeDtypeStruct((XN, NQB * 16, STATE), BF16),
        in_specs=[in_smem(), in_vmem(), in_smem()] + [in_hbm()] * 4,
        out_specs=in_vmem(),
        scratch_shapes=state_scratch(XN - 1, 2 * cache[0].shape[0]),
        compiler_params=pltpu.CompilerParams(vmem_limit_bytes=VMEM_LIMIT),
        cost_estimate=attend_cost(XN - 1),
    )(where, q, listed, *cache)


def weights_of(stats):
    tops = [s[:, :GROUP] for s in stats]
    peak = tops[0]
    for t in tops[1:]:
        peak = jnp.maximum(peak, t)
    weights = [jnp.exp2(t - peak) for t in tops]
    total = None
    for w, s in zip(weights, stats):
        term = w * (s[:, GROUP : 2 * GROUP] + s[:, 2 * GROUP : 3 * GROUP])
        total = term if total is None else total + term
    return peak, weights, total


def merge_kernel(place_ref, own_ref, in_ref, out_ref):
    rows = own_ref.shape[0]
    column = place_ref[0]
    sources = [own_ref] + [in_ref.at[lax.rem(column + j, XN)] for j in range(1, XN)]
    peak, weights, total = weights_of([s[:, WIDE:].astype(F32) for s in sources])
    for h in range(GROUP):
        cols = slice(h * DH, (h + 1) * DH)
        value = None
        for source, weight in zip(sources, weights):
            term = source[:, cols].astype(F32) * weight[:, h : h + 1]
            value = term if value is None else value + term
        out_ref[:, cols] = value.astype(BF16)
    high = total.astype(BF16).astype(F32)
    rest = jnp.zeros((rows, 128 - 3 * GROUP), F32)
    out_ref[:, WIDE:] = jnp.concatenate([peak, high, total - high, rest], axis=1).astype(BF16)


def merge(where, own, states):
    return pl.pallas_call(
        merge_kernel,
        name="merge",
        out_shape=jax.ShapeDtypeStruct(states.shape[1:], BF16),
        in_specs=[in_smem(), in_vmem(), in_vmem()],
        out_specs=in_vmem(),
        compiler_params=pltpu.CompilerParams(vmem_limit_bytes=VMEM_LIMIT),
    )(where, own, states)


def finish_kernel(in_ref, out_ref):
    pairs = in_ref.shape[0] // 16
    stats = []
    for i in range(pairs):
        both = in_ref[i * 16 : (i + 1) * 16, WIDE:].astype(F32)
        stats += [both[:ROWS], both[ROWS:]]
    _, weights, total = weights_of(stats)
    inverse = 1.0 / total
    weights = [w * inverse for w in weights]
    for h in range(GROUP):
        cols = slice(h * DH, (h + 1) * DH)
        value = None
        for i in range(pairs):
            both = in_ref[i * 16 : (i + 1) * 16, cols].astype(F32)
            term = (
                both[:ROWS] * weights[2 * i][:, h : h + 1]
                + both[ROWS:] * weights[2 * i + 1][:, h : h + 1]
            )
            value = term if value is None else value + term
        twice = jnp.concatenate([value, value], axis=0).astype(BF16)
        for i in range(out_ref.shape[0] // 16):
            out_ref[i * 16 : (i + 1) * 16, cols] = twice


def finish(states):
    return pl.pallas_call(
        finish_kernel,
        out_shape=jax.ShapeDtypeStruct((ZN // 2 * ROWS, WIDE), BF16),
        in_specs=[in_vmem()],
        out_specs=in_vmem(),
        compiler_params=pltpu.CompilerParams(vmem_limit_bytes=VMEM_LIMIT),
    )(states)


def project_kernel(core_ref, a_ref, w0_ref, w1_ref, out_ref):
    core = core_ref[0]
    rows = a_ref[...].reshape(XN * ZN * ROWS, WIDE)
    for side, w_ref in enumerate((w0_ref, w1_ref)):
        result = jnp.dot(rows, w_ref[...], preferred_element_type=F32)
        target = core if side == 0 else 1 - core
        for w in range(ZN):
            pair, low = w // 2, w % 2
            starts = [((low * XN + x) * (ZN // 2) + pair) * ROWS for x in range(XN)]
            chunk = jnp.concatenate([result[start : start + ROWS] for start in starts], axis=0)
            out_ref[target, lax.rem(w + core + target * (YN // 2), ZN)] = chunk.astype(BF16)


def project(core, rows, w0, w1):
    return pl.pallas_call(
        project_kernel,
        out_shape=jax.ShapeDtypeStruct((2, ZN, XN * ROWS, w0.shape[1]), BF16),
        in_specs=[in_smem()] + [in_vmem()] * 3,
        out_specs=in_vmem(),
        compiler_params=pltpu.CompilerParams(vmem_limit_bytes=VMEM_LIMIT),
    )(core, rows, w0, w1)


def find_hits(block_slots, selected, device, head, local_blocks):
    chosen = lax.dynamic_index_in_dim(selected, head, 0, keepdims=False)
    pair = lax.dynamic_slice_in_dim(block_slots, device // 2 * 2 * local_blocks, 2 * local_blocks)
    pair = pair.reshape(2, local_blocks)
    logical = jnp.where(device % 2 == 0, pair, pair[::-1]).reshape(-1)
    hit = jnp.any(chosen[:, None, :] == logical[None, :, None], axis=2).astype(jnp.int32)
    last = (logical == block_slots.shape[0] - 1).astype(jnp.int32)
    return hit * (1 + last[None, :])


def body(queries, keys, values, block_slots, selected, out_weight):
    device = lax.axis_index("ctx")
    head = lax.axis_index("kvh")
    core = (device % 2).reshape(1).astype(jnp.int32)
    where = jnp.stack([device // 2 % XN, device % 2]).astype(jnp.int32)
    hits = find_hits(block_slots, selected, device, head, keys.shape[0] // BLKSZ)
    other_keys = lax.ppermute(keys, "ctx", CORE_SWAP)
    other_values = lax.ppermute(values, "ctx", CORE_SWAP)

    column = spread(queries, "ctx", Z_GROUPS).reshape(ZN * ROWS, WIDE)
    cache = (keys, values, other_keys, other_values)
    own, listed = attend_own(where, column.reshape(NQB, 16, WIDE), hits, cache)
    plane = spread(column, "ctx", X_GROUPS).reshape(XN, NQB, 16, WIDE)
    states = attend_rest(where, plane, listed, cache)
    states, out_weight = lax.optimization_barrier((states, out_weight))
    other_weight = lax.ppermute(out_weight, "ctx", CORE_SWAP)
    merged = merge(where, own, exchange(states, "ctx", X_GROUPS))
    arrived = exchange(merged.reshape(ZN, ROWS, STATE), "ctx", Z_GROUPS)
    attended = finish(arrived.reshape(ZN * ROWS, STATE)).reshape(ZN // 2, ROWS, WIDE)

    column = exchange(attended, "ctx", FAR_GROUPS).reshape(ZN // 2 * ROWS, WIDE)
    plane = spread(column, "ctx", NEAR_GROUPS)
    shares = project(core, plane, out_weight, other_weight)
    arrived = exchange(shares.reshape(2 * YN, XN * ROWS, -1), ("ctx", "kvh"), YC_GROUPS)
    summed = jnp.sum(arrived.reshape(2, YN, XN, ROWS, -1).astype(F32), axis=1)
    return jnp.swapaxes(summed, 0, 1).reshape(XN * 2 * ROWS, -1)


def solution(mesh):
    return jax.shard_map(
        body,
        mesh=mesh,
        in_specs=(P("ctx", "kvh"), P("ctx", "kvh"), P("ctx", "kvh"), P(), P(), P("kvh", "ctx")),
        out_specs=P("kvh", "ctx"),
        check_vma=False,
    )
```
